32 devices in a mesh: tok: 8 (over z, y), feat: 4 (over x, core).
Axes of the slice: x: 2, y: 2, z: 4, core: 2. Of those that a mesh axis runs over, the one named last changes fastest.
Arguments:
- activations: bfloat16 [12288, 8192], P('tok', 'feat'), as said below
- start_basis: float32 [32, 8192], P(None, 'feat'), may hold values from -6 to 6
Outputs:
- scores: float32 [12288], P('tok')
- basis: float32 [32, 8192], P(None, 'feat')
The draws below stay inside these ranges and needn't reach their ends.
Inputs may be any that keep to these rules, and one draw needn't show every extreme that they name: `activations`: token rows carry a feature offset whose size varies along the rows, on top of independent entries.
All inputs are finite; a program needn't handle non-finite values.
Results may differ from the reference program's by a relative error of at most 0.0048.
Values may be sent and summed in bfloat16 or wider, within the bound.
No kernel may reach another device: no remote copies, remote signals or barrier semaphores. Data moves between devices by JAX's collectives and lax.ppermute only.
A program may use at most 64 MiB of HBM per device.

```python
import jax
import jax.numpy as jnp
from jax import lax

D = 8192
K = 32
ITERS = 4
TOK_DEV = 1536
ROWS = 12288
N_TOK = 8


def draw_activations(key, part):
    key_noise = jax.random.fold_in(key, 11)
    key_offset = jax.random.fold_in(key, 12)
    offset = jax.random.uniform(key_offset, (D,), jnp.float32, -0.1, 0.1)
    position = jnp.arange(ROWS, dtype=jnp.float32) / (ROWS - 1)
    ramp = jnp.exp(2.3025851 * position)
    noise = jax.random.normal(key_noise, (ROWS, D), jnp.float32)
    return (noise + ramp[:, None] * offset[None, :]).astype(jnp.bfloat16)


def shard_levels(key, dims, pieces, smallest, top_value):
    level, own = 1.0, jax.random.fold_in(key, 6)
    for dim, shards_of in pieces:
        draws = jnp.exp(jax.random.uniform(jax.random.fold_in(own, dim), (shards_of,), jnp.float32, smallest / len(pieces), top_value / len(pieces)))
        level = level * jnp.repeat(draws, dims[dim] // shards_of).reshape([-1 if axis == dim else 1 for axis in range(len(dims))])
    return level


def gaussian(key, extent, deviation, bound, pieces=(), held_as=jnp.bfloat16):
    entries = deviation * jax.random.normal(key, extent, jnp.float32)
    if pieces:
        entries = entries * shard_levels(key, extent, pieces, -0.22, 0.18)
    return jnp.clip(entries, -bound, bound).astype(held_as)


def setup_inputs(seed: int = 0) -> dict:
    streams_of = jax.random.split(jax.random.key(seed), 3)
    activations = draw_activations(jax.random.fold_in(streams_of[2], 71), 0)
    start_basis = gaussian(streams_of[1], (K, D), 1.0, 6.0, ((1, 4),), jnp.float32)
    return {"activations": activations, "start_basis": start_basis}


def project(activations, vectors, mean):
    shift = jnp.dot(vectors.astype(jnp.float32), mean, precision=lax.Precision.HIGHEST)
    blocks = activations.reshape(N_TOK, TOK_DEV, D)

    def single(block):
        product = lax.dot_general(vectors.astype(jnp.float32), block.astype(jnp.float32), (((1,), (1,)), ((), ())), preferred_element_type=jnp.float32)
        return product - shift[:, None]
    return lax.map(single, blocks)

def image_of(activations, weights, mean):
    blocks = activations.reshape(N_TOK, TOK_DEV, D)

    def accumulate(total, pair):
        block, weight_block = pair
        term = jnp.dot(weight_block.astype(jnp.float32), block.astype(jnp.float32), preferred_element_type=jnp.float32)
        counts = jnp.sum(weight_block.astype(jnp.float32), axis=1)
        return (total + term - counts[:, None] * mean[None, :], None)
    total, _ = lax.scan(accumulate, jnp.zeros((K, D), jnp.float32), (blocks, weights))
    return total

def reference(activations, start_basis):
    mean = jnp.sum(activations, axis=0, dtype=jnp.float32) / ROWS
    basis = start_basis
    for step in range(ITERS):
        vectors = basis.astype(jnp.bfloat16)
        projected = project(activations, vectors, mean)
        weights = projected.astype(jnp.bfloat16)
        image = image_of(activations, weights, mean)
        gram = jnp.dot(image, image.T, precision=lax.Precision.HIGHEST)
        lower = jnp.linalg.cholesky(gram)
        basis = jax.scipy.linalg.solve_triangular(lower, image, lower=True)
    projected = project(activations, basis.astype(jnp.bfloat16), mean)
    scores = jnp.mean(projected * projected, axis=1).reshape(ROWS)
    return (scores, basis)
```

```python
import functools

import jax
import jax.numpy as jnp
from jax import lax
from jax.experimental import pallas as pl
from jax.experimental.pallas import tpu as pltpu
from jax.sharding import PartitionSpec as P

ITERS = 4
PEERS = 4
LANES = 128
HIGHEST = lax.Precision.HIGHEST
VMEM = pl.BlockSpec(memory_space=pltpu.VMEM)
SMEM = pl.BlockSpec(memory_space=pltpu.SMEM)
F32 = jnp.float32
BF16 = jnp.bfloat16


def call(kernel, outputs, name, scratch=()):
    def run(*args):
        specs = [SMEM if arg.dtype == jnp.int32 else VMEM for arg in args]
        return pl.pallas_call(
            kernel,
            out_shape=[jax.ShapeDtypeStruct(shape, F32) for shape in outputs],
            in_specs=specs,
            out_specs=[VMEM] * len(outputs),
            scratch_shapes=scratch,
            compiler_params=pltpu.CompilerParams(vmem_limit_bytes=20 * 2**20),
            name=name,
        )(*args)

    return run


def split(value):
    high = value.astype(BF16)
    low = (value - high.astype(F32)).astype(BF16)
    return jnp.concatenate([high, low], axis=0)


def join(value):
    half = value.shape[0] // 2
    return value[:half] + value[half:]


def contract_last(left, right, precision=None):
    return lax.dot_general(
        left, right, (((1,), (1,)), ((), ())), preferred_element_type=F32, precision=precision
    )


def column_sums_kernel(rows_ref, sums_ref):
    ones = jnp.ones((16, rows_ref.shape[0]), BF16)
    sums_ref[...] = jnp.dot(ones, rows_ref[...], preferred_element_type=F32)[:1]


def first_projection_kernel(basis_ref, rows_ref, out_ref):
    tokens = rows_ref.shape[0]
    out_ref[:, :tokens] = join(contract_last(split(basis_ref[...]), rows_ref[...]))
    out_ref[:, tokens:] = jnp.zeros((out_ref.shape[0], LANES), F32)


def projection_kernel(me_ref, c0, c1, c2, c3, mean_ref, rows_ref, out_ref, image_ref):
    tokens = rows_ref.shape[0]
    width = c0.shape[1]
    for distance, chunk in enumerate((c0, c1, c2, c3)):
        place = pl.multiple_of((me_ref[0] ^ distance) * width, width)
        image_ref[:, pl.ds(place, width)] = chunk[...]
    image = image_ref[...]
    shift = jnp.sum(image * mean_ref[...], axis=1, keepdims=True)
    out_ref[:, :tokens] = join(contract_last(split(image), rows_ref[...])) - shift
    out_ref[:, tokens:] = jnp.zeros((out_ref.shape[0], LANES), F32)
    out_ref[:, tokens : tokens + out_ref.shape[0]] = contract_last(image, image, HIGHEST)


def inverse_factor(gram):
    n = gram.shape[0]
    row = lax.broadcasted_iota(jnp.int32, (n, n), 0)
    column = lax.broadcasted_iota(jnp.int32, (n, n), 1)
    work = jnp.concatenate([gram, (row == column).astype(F32)], axis=1)
    below = lax.broadcasted_iota(jnp.int32, (n, 1), 0)
    scale = jnp.zeros((n, 1), F32)
    for k in range(n):
        pivot_row = work[k : k + 1, :]
        pivot = work[k : k + 1, k : k + 1]
        factor = jnp.where(below > k, work[:, k : k + 1] / pivot, 0.0)
        scale = jnp.where(below == k, lax.rsqrt(pivot), scale)
        work = work - factor * pivot_row
    return work[:, n:] * scale


def image_kernel(first, me_ref, own_ref, got_ref, mean_ref, sums_ref, rows_ref, o0, o1, o2, o3):
    tokens = rows_ref.shape[0]
    width = o0.shape[1]
    n = own_ref.shape[0]
    projected = own_ref[:, :tokens] + got_ref[:, :tokens]
    if first:
        centre = jnp.sum(projected, axis=1, keepdims=True) / tokens
        projected = projected - centre
    else:
        gram = own_ref[:, tokens:] + got_ref[:, tokens:]
        lower = inverse_factor(gram[:, :n])
        projected = jnp.dot(lower, projected, preferred_element_type=F32, precision=HIGHEST)
    weights = split(projected)
    counts = join(jnp.sum(weights.astype(F32), axis=1, keepdims=True))
    for distance, out in enumerate((o0, o1, o2, o3)):
        place = pl.ds(pl.multiple_of((me_ref[0] ^ distance) * width, width), width)
        mean = mean_ref[:, place]
        term = join(jnp.dot(weights, rows_ref[:, place], preferred_element_type=F32))
        term = term - counts * mean
        if first:
            term = term + centre * (sums_ref[:, place] - tokens * mean)
        out[...] = term


def last_kernel(own_ref, got_ref, image_ref, scores_ref, basis_ref):
    n = own_ref.shape[0]
    tokens = own_ref.shape[1] - LANES
    total = own_ref[...] + got_ref[...]
    lower = inverse_factor(total[:, tokens : tokens + n])
    projected = jnp.dot(lower, total[:, :tokens], preferred_element_type=F32, precision=HIGHEST)
    scores_ref[...] = jnp.sum(projected * projected, axis=0, keepdims=True) / n
    basis_ref[...] = jnp.dot(lower, image_ref[...], preferred_element_type=F32, precision=HIGHEST)


def add_kernel(*refs):
    terms = [ref[...] for ref in refs[:-1]]
    while len(terms) > 1:
        terms = [sum(terms[i + 1 : i + 2], terms[i]) for i in range(0, len(terms), 2)]
    refs[-1][...] = terms[0]


def add(*terms):
    return call(add_kernel, [terms[0].shape], "add")(*terms)[0]


def swap(value, axis, distance):
    size = lax.axis_size(axis)
    return lax.ppermute(value, axis, [(i, i ^ distance) for i in range(size)])


def distances(axis, start):
    step, size = start, lax.axis_size(axis)
    while step < size:
        yield step
        step *= 2


def sum_but_last(value, axis):
    steps = list(distances(axis, 1))
    for step in steps[:-1]:
        value = add(value, swap(value, axis, step))
    return value, swap(value, axis, steps[-1])


def share(value, axis):
    return [value] + [swap(value, axis, d) for d in range(1, PEERS)]


def on_device(activations, start_basis):
    tokens, features = activations.shape
    n = start_basis.shape[0]
    width = features // PEERS
    me = (lax.axis_index("tok") % PEERS).astype(jnp.int32).reshape(1)
    total_rows = tokens * lax.axis_size("tok")

    sums = call(column_sums_kernel, [(1, features)], "column_sums")(activations)[0]
    all_sums = add(*share(sums, "tok"))
    for step in distances("tok", PEERS):
        all_sums = add(all_sums, swap(all_sums, "tok", step))
    mean = all_sums / total_rows

    packed = (n, tokens + LANES)
    partial = call(first_projection_kernel, [packed], "first_projection")(start_basis, activations)[0]
    for step in range(ITERS):
        own, got = sum_but_last(partial, "feat")
        kernel = functools.partial(image_kernel, step == 0)
        terms = call(kernel, [(n, width)] * PEERS, "image")(me, own, got, mean, sums, activations)
        received = [swap(term, "tok", d) for d, term in enumerate(terms) if d]
        chunk = add(terms[0], *received)
        for distance in distances("tok", PEERS):
            chunk = add(chunk, swap(chunk, "tok", distance))
        partial, image = call(projection_kernel, [packed, (n, features)], "projection")(
            me, *share(chunk, "tok"), mean, activations
        )
    own, got = sum_but_last(partial, "feat")
    scores, basis = call(last_kernel, [(1, tokens), (n, features)], "last")(own, got, image)
    return (scores.reshape(tokens), basis)


def solution(mesh):
    in_specs = (P("tok", "feat"), P(None, "feat"))
    out_specs = (P("tok"), P(None, "feat"))
    return jax.shard_map(
        on_device, mesh=mesh, in_specs=in_specs, out_specs=out_specs, check_vma=False
    )
```

```python
import functools

import jax
import jax.numpy as jnp
from jax import lax
from jax.experimental import pallas as pl
from jax.experimental.pallas import tpu as pltpu
from jax.sharding import PartitionSpec as P

ITERS = 4
PEERS = 4
LANES = 128
EXTRA = 8
LONG = pl.CostEstimate(flops=2**34, bytes_accessed=0, transcendentals=0)
SHORT = pl.CostEstimate(flops=2**29, bytes_accessed=0, transcendentals=0)
HIGHEST = lax.Precision.HIGHEST
VMEM = pl.BlockSpec(memory_space=pltpu.VMEM)
HBM = pl.BlockSpec(memory_space=pltpu.HBM)
F32 = jnp.float32
BF16 = jnp.bfloat16


def call(kernel, outputs, name, scratch=(), in_specs=None, mebibytes=20, cost=None):
    def run(*args):
        specs = in_specs or [VMEM] * len(args)
        return pl.pallas_call(
            kernel,
            out_shape=[jax.ShapeDtypeStruct(shape, dtype) for shape, dtype in outputs],
            in_specs=specs,
            out_specs=[VMEM] * len(outputs),
            scratch_shapes=scratch,
            compiler_params=pltpu.CompilerParams(vmem_limit_bytes=mebibytes * 2**20),
            cost_estimate=cost,
            name=name,
        )(*args)

    return run


def split(value):
    high = value.astype(BF16)
    low = (value - high.astype(F32)).astype(BF16)
    return jnp.concatenate([high, low], axis=0)


def join(value):
    half = value.shape[0] // 2
    return value[:half] + value[half:]


def total(*refs):
    terms = [ref[...].astype(F32) for ref in refs]
    while len(terms) > 1:
        terms = [sum(terms[i + 1 : i + 2], terms[i]) for i in range(0, len(terms), 2)]
    return terms[0]


def contract_last(left, right, precision=None):
    return lax.dot_general(
        left, right, (((1,), (1,)), ((), ())), preferred_element_type=F32, precision=precision
    )


def position():
    return lax.rem(lax.axis_index("tok"), PEERS)


def diagonal(n):
    return lax.broadcasted_iota(jnp.int32, (n, n), 0) == lax.broadcasted_iota(jnp.int32, (n, n), 1)


def first_projection_kernel(blocks, basis_hbm, rows_hbm, out_ref, rows_ref, basis_ref, sems):
    tokens = rows_ref.shape[0]
    height = tokens // blocks
    fetch_basis = pltpu.make_async_copy(basis_hbm, basis_ref, sems.at[blocks])
    fetch_basis.start()
    fetches = []
    for i in range(blocks):
        place = pl.ds(i * height, height)
        fetches.append(
            pltpu.make_async_copy(rows_hbm.at[place, :], rows_ref.at[place, :], sems.at[i])
        )
        fetches[-1].start()
    fetch_basis.wait()
    vectors = split(basis_ref[...])
    for i in range(blocks):
        fetches[i].wait()
        place = pl.ds(i * height, height)
        out_ref[:, place] = join(contract_last(vectors, rows_ref[place, :]))


def projection_kernel(part, first, *refs):
    chunk_ref, rows_ref, *refs = refs
    mean_ref = chunk_ref if first else refs.pop(0)
    n, width = mean_ref.shape[0] - EXTRA, chunk_ref.shape[1]
    place = pl.ds(pl.multiple_of((position() ^ part) * width, width), width)
    chunk = chunk_ref[:n, :]
    shift = jnp.sum(chunk * mean_ref[n : n + 1, :], axis=1, keepdims=True)
    projected = join(contract_last(split(chunk), rows_ref[:, place])) - shift
    gram = contract_last(chunk, chunk, HIGHEST)
    if part > 0:
        projected = refs.pop(0)[...] + projected
    if part == 1:
        gram = refs.pop(0)[...] + gram
    if part < PEERS - 1:
        refs[0][...] = projected
        refs[1][...] = gram
        return
    gram = refs[0][...] + (refs[1][...] + gram)
    out_ref, tokens = refs[2], rows_ref.shape[0]
    out_ref[:, :tokens] = projected
    out_ref[:, tokens:] = jnp.zeros((n, LANES), F32)
    out_ref[:, tokens : tokens + n] = gram


def inverse_factor_kernel(own_ref, got_ref, out_ref):
    n = own_ref.shape[0]
    gram = (own_ref[...] + got_ref[...])[:, :n]
    work = jnp.concatenate([gram, diagonal(n).astype(F32)], axis=1)
    index = lax.broadcasted_iota(jnp.int32, (n, 1), 0)
    scale = jnp.zeros((n, 1), F32)
    for k in range(0, n, 2):
        row0, row1 = work[k : k + 1, :], work[k + 1 : k + 2, :]
        column0, column1 = work[:, k : k + 1], work[:, k + 1 : k + 2]
        pivot0, beside = row0[:, k : k + 1], row0[:, k + 1 : k + 2]
        inverse0 = 1.0 / pivot0
        share0 = beside * inverse0
        pivot1 = row1[:, k + 1 : k + 2] - share0 * beside
        inverse1 = 1.0 / pivot1
        row1 = row1 - share0 * row0
        factor0 = column0 * inverse0
        factor1 = jnp.where(index > k + 1, (column1 - factor0 * beside) * inverse1, 0.0)
        factor0 = jnp.where(index > k, factor0, 0.0)
        scale = jnp.where(index == k, lax.rsqrt(pivot0), scale)
        scale = jnp.where(index == k + 1, lax.rsqrt(pivot1), scale)
        work = work - factor0 * row0 - factor1 * row1
    out_ref[...] = work[:, n:] * scale


def first_term(weights, rows, counts, centre, out_ref):
    n, width = counts.shape[0], out_ref.shape[1]
    term = jnp.dot(weights, rows, preferred_element_type=F32)
    sums = term[2 * n : 2 * n + 1]
    out_ref[:n, :] = join(term[: 2 * n]) + centre * sums
    out_ref[n:, :] = jnp.zeros((EXTRA, width), F32)
    out_ref[n : n + 1, :] = sums
    counts = jnp.where(diagonal(n), counts, 0.0)
    out_ref[n + 1 : n + 2, :n] = jnp.sum(counts, axis=0, keepdims=True)


def first_image_kernel(own_ref, got_ref, rows_ref, *outs):
    *outs, weights_ref, side_ref = outs
    tokens, n, width = rows_ref.shape[0], own_ref.shape[0], outs[0].shape[1]
    projected = total(own_ref, got_ref)[:, :tokens]
    centre = [jnp.sum(ref[:, tokens:].astype(F32), axis=1, keepdims=True) for ref in (own_ref, got_ref)]
    centre = centre[0] + centre[1]
    weights = split(projected)
    counts = join(jnp.sum(weights.astype(F32), axis=1, keepdims=True)) + centre * tokens
    weights = jnp.concatenate([weights, jnp.ones((2 * EXTRA, tokens), BF16)], axis=0)
    for part, out in enumerate(outs, 1):
        place = pl.ds(pl.multiple_of((position() ^ part) * width, width), width)
        first_term(weights, rows_ref[:, place], counts, centre, out)
    weights_ref[...] = weights
    side_ref[...] = jnp.broadcast_to(counts, side_ref.shape)
    side_ref[:, 1:2] = centre


def first_own_image_kernel(weights_ref, side_ref, rows_ref, out_ref):
    width = out_ref.shape[1]
    place = pl.ds(pl.multiple_of(position() * width, width), width)
    first_term(weights_ref[...], rows_ref[:, place], side_ref[:, :1], side_ref[:, 1:2], out_ref)


def first_total_kernel(rows_in_all, own_ref, got_ref, out_ref):
    n = own_ref.shape[0] - EXTRA
    value = own_ref[...] + got_ref[...]
    mean = value[n : n + 1] / rows_in_all
    counts = jnp.where(diagonal(n), value[n + 1 : n + 2, :n], 0.0)
    counts = jnp.sum(counts, axis=1, keepdims=True)
    out_ref[:n, :] = value[:n] - counts * mean
    out_ref[n:, :] = jnp.broadcast_to(mean, (EXTRA, mean.shape[1]))


def image_kernel(own_ref, got_ref, lower_ref, rows_ref, *refs):
    means, outs, (weights_ref, side_ref) = refs[: PEERS - 1], refs[PEERS - 1 : -2], refs[-2:]
    n, width = own_ref.shape[0], outs[0].shape[1]
    projected = total(own_ref, got_ref)
    projected = jnp.dot(lower_ref[...], projected, preferred_element_type=F32, precision=HIGHEST)
    weights = split(projected)
    counts = join(jnp.sum(weights.astype(F32), axis=1, keepdims=True))
    for part, (mean, out) in enumerate(zip(means, outs), 1):
        place = pl.ds(pl.multiple_of((position() ^ part) * width, width), width)
        term = join(jnp.dot(weights, rows_ref[:, place], preferred_element_type=F32))
        out[...] = term - counts * mean[n : n + 1, :]
    weights_ref[...] = weights
    side_ref[...] = jnp.broadcast_to(counts, side_ref.shape)


def own_image_kernel(weights_ref, side_ref, rows_ref, mean_ref, out_ref):
    n, width = out_ref.shape
    place = pl.ds(pl.multiple_of(position() * width, width), width)
    term = join(jnp.dot(weights_ref[...], rows_ref[:, place], preferred_element_type=F32))
    out_ref[...] = term - side_ref[:, :1] * mean_ref[n : n + 1, :]


def assemble_kernel(c0, c1, c2, c3, out_ref):
    n, width = out_ref.shape[0], c0.shape[1]
    for part, chunk in enumerate((c0, c1, c2, c3)):
        place = pl.ds(pl.multiple_of((position() ^ part) * width, width), width)
        out_ref[:, place] = chunk[:n, :]


def last_kernel(own_ref, got_ref, lower_ref, image_ref, scores_ref, basis_ref):
    n = own_ref.shape[0]
    lower = lower_ref[...]
    basis_ref[...] = jnp.dot(lower, image_ref[...], preferred_element_type=F32, precision=HIGHEST)
    projected = total(own_ref, got_ref)
    projected = jnp.dot(lower, projected, preferred_element_type=F32, precision=HIGHEST)
    scores_ref[...] = jnp.sum(projected * projected, axis=0) / n


def add_kernel(*refs):
    refs[-1][...] = total(*refs[:-1])


def add(*terms):
    return call(add_kernel, [(terms[0].shape, F32)], "add")(*terms)[0]


def part_kernel(*refs):
    *terms, projected_ref, gram_ref = refs
    tokens = projected_ref.shape[1]
    value = total(*terms)
    projected_ref[...] = value[:, :tokens].astype(projected_ref.dtype)
    gram_ref[...] = value[:, tokens:]


def first_part_kernel(*refs):
    *terms, out_ref = refs
    tokens = out_ref.shape[1] - LANES
    value = total(*terms)
    centre = jnp.sum(value, axis=1, keepdims=True) / tokens
    out_ref[:, :tokens] = (value - centre).astype(BF16)
    out_ref[:, tokens:] = jnp.zeros((value.shape[0], LANES), BF16)
    for lane in range(3):
        term = centre.astype(BF16)
        out_ref[:, tokens + lane : tokens + lane + 1] = term
        centre = centre - term.astype(F32)


def swap(value, axis, distance):
    size = lax.axis_size(axis)
    return lax.ppermute(value, axis, [(i, i ^ distance) for i in range(size)])


def distances(axis, start):
    step, size = start, lax.axis_size(axis)
    while step < size:
        yield step
        step *= 2


def sum_but_last(value, axis):
    terms = [value]
    for step in list(distances(axis, 1))[:-1]:
        terms = [add(*terms)] if len(terms) > 1 else terms
        terms.append(swap(terms[0], axis, step))
    return terms


def share(value, axis):
    return [value] + [swap(value, axis, d) for d in range(1, PEERS)]


def on_device(activations, start_basis):
    tokens, features = activations.shape
    n = start_basis.shape[0]
    width = features // PEERS
    rows_in_all = tokens * lax.axis_size("tok")
    last_feat = lax.axis_size("feat") // 2

    blocks = 3
    partial, rows = call(
        functools.partial(first_projection_kernel, blocks),
        [((n, tokens), F32), (activations.shape, BF16)],
        "first_projection",
        scratch=[pltpu.VMEM((n, features), F32), pltpu.SemaphoreType.DMA((blocks + 1,))],
        in_specs=[HBM, HBM],
        mebibytes=46,
    )(start_basis, activations)
    terms = sum_but_last(partial, "feat")
    own = call(first_part_kernel, [((n, tokens + LANES), BF16)], "first_part")(*terms)[0]
    got = swap(own, "feat", last_feat)
    packed, side = ((n, tokens + LANES), F32), ((n, LANES), F32)
    for step in range(ITERS):
        first = step == 0
        chunk = ((n + EXTRA if first else n, width), F32)
        weights = ((2 * n + 2 * EXTRA if first else 2 * n, tokens), BF16)
        outputs = [chunk] * (PEERS - 1) + [weights, side]
        if first:
            *terms, weights, sums = call(first_image_kernel, outputs, "first_image")(own, got, rows)
            received = [swap(term, "tok", d) for d, term in enumerate(terms, 1)]
            kept = call(first_own_image_kernel, [chunk], "first_own_image", cost=SHORT)(weights, sums, rows)
        else:
            *terms, weights, sums = call(image_kernel, outputs, "image")(own, got, lower, rows, *means[1:])
            received = [swap(term, "tok", d) for d, term in enumerate(terms, 1)]
            kept = call(own_image_kernel, [chunk], "own_image", cost=SHORT)(weights, sums, rows, means[0])
        image = add(*kept, *received)
        *steps, last_step = distances("tok", PEERS)
        for distance in steps:
            image = add(image, swap(image, "tok", distance))
        kernel = functools.partial(first_total_kernel, rows_in_all) if first else add_kernel
        image = call(kernel, [chunk], "total")(image, swap(image, "tok", last_step))[0]
        images = share(image, "tok")
        if first:
            means = images
        before = []
        for part, image in enumerate(images):
            last = part == PEERS - 1
            operands = [image, rows] + ([] if first else [means[part]])
            operands += [projected] if part else []
            operands += before[:1] if part == 1 else before[1:] if last else []
            projected, *gram = call(
                functools.partial(projection_kernel, part, first),
                [packed] if last else [((n, tokens), F32), ((n, n), F32)],
                "projection",
                cost=SHORT,
            )(*operands)
            before += gram
        terms = sum_but_last(projected, "feat")
        sent = BF16 if step == ITERS - 1 else F32
        own, gram = call(part_kernel, [((n, tokens), sent), side], "part")(*terms)
        got_gram = swap(gram, "feat", last_feat)
        got = swap(own, "feat", last_feat)
        lower = call(inverse_factor_kernel, [((n, n), F32)], "inverse_factor", cost=LONG)(gram, got_gram)[0]
    image = call(assemble_kernel, [((n, features), F32)], "assemble")(*images)[0]
    outputs = [((tokens,), F32), ((n, features), F32)]
    return tuple(call(last_kernel, outputs, "last")(own, got, lower, image))


def solution(mesh):
    in_specs = (P("tok", "feat"), P(None, "feat"))
    out_specs = (P("tok"), P(None, "feat"))
    return jax.shard_map(
        on_device, mesh=mesh, in_specs=in_specs, out_specs=out_specs, check_vma=False
    )
```

```python
import functools

import jax
import jax.numpy as jnp
from jax import lax
from jax.experimental import pallas as pl
from jax.experimental.pallas import tpu as pltpu
from jax.sharding import PartitionSpec as P

ITERS = 4
PEERS = 4
LANES = 128
EXTRA = 8
ORDER = (0, 3, 1, 2)
TERMS = 3
LONG = pl.CostEstimate(flops=2**34, bytes_accessed=0, transcendentals=0)
SHORT = pl.CostEstimate(flops=2**29, bytes_accessed=0, transcendentals=0)
HIGHEST = lax.Precision.HIGHEST
VMEM = pl.BlockSpec(memory_space=pltpu.VMEM)
HBM = pl.BlockSpec(memory_space=pltpu.HBM)
F32 = jnp.float32
BF16 = jnp.bfloat16


def call(kernel, outputs, name, scratch=(), in_specs=None, mebibytes=20, cost=None):
    def run(*args):
        specs = in_specs or [VMEM] * len(args)
        return pl.pallas_call(
            kernel,
            out_shape=[jax.ShapeDtypeStruct(shape, dtype) for shape, dtype in outputs],
            in_specs=specs,
            out_specs=[VMEM] * len(outputs),
            scratch_shapes=scratch,
            compiler_params=pltpu.CompilerParams(vmem_limit_bytes=mebibytes * 2**20),
            cost_estimate=cost,
            name=name,
        )(*args)

    return run


def split(value, terms=2):
    parts = []
    for _ in range(terms):
        parts.append(value.astype(BF16))
        value = value - parts[-1].astype(F32)
    return jnp.concatenate(parts, axis=0)


def join(value, terms=2):
    height = value.shape[0] // terms
    result = value[-height:]
    for term in range(terms - 2, -1, -1):
        result = value[term * height : (term + 1) * height] + result
    return result


def total(*refs):
    terms = [ref[...].astype(F32) for ref in refs]
    while len(terms) > 1:
        terms = [sum(terms[i + 1 : i + 2], terms[i]) for i in range(0, len(terms), 2)]
    return terms[0]


def contract_last(left, right, precision=None):
    return lax.dot_general(
        left, right, (((1,), (1,)), ((), ())), preferred_element_type=F32, precision=precision
    )


def position():
    return lax.rem(lax.axis_index("tok"), PEERS)


def diagonal(n):
    return lax.broadcasted_iota(jnp.int32, (n, n), 0) == lax.broadcasted_iota(jnp.int32, (n, n), 1)


def first_projection_kernel(blocks, basis_hbm, rows_hbm, out_ref, rows_ref, basis_ref, sems):
    tokens = rows_ref.shape[0]
    height = tokens // blocks
    fetch_basis = pltpu.make_async_copy(basis_hbm, basis_ref, sems.at[blocks])
    fetch_basis.start()
    fetches = []
    for i in range(blocks):
        place = pl.ds(i * height, height)
        fetches.append(
            pltpu.make_async_copy(rows_hbm.at[place, :], rows_ref.at[place, :], sems.at[i])
        )
        fetches[-1].start()
    fetch_basis.wait()
    vectors = split(basis_ref[...])
    for i in range(blocks):
        fetches[i].wait()
        place = pl.ds(i * height, height)
        out_ref[:, place] = join(contract_last(vectors, rows_ref[place, :]))


def core():
    return lax.rem(lax.axis_index("feat"), 2)


def chunk_gram(chunk_ref, n):
    chunk = chunk_ref[:n, :]
    return contract_last(chunk, chunk, HIGHEST)


def projection_kernel(part, first, chunk_ref, rows_ref, *refs):
    mean_ref, refs = (chunk_ref, refs) if first else (refs[0], refs[1:])
    n, width = mean_ref.shape[0] - EXTRA, chunk_ref.shape[1]
    place = pl.ds(pl.multiple_of((position() ^ part) * width, width), width)
    chunk = chunk_ref[:n, :]
    shift = jnp.sum(chunk * mean_ref[n : n + 1, :], axis=1, keepdims=True)
    projected = join(contract_last(split(chunk), rows_ref[:, place])) - shift
    if part != ORDER[0]:
        projected = refs[0][...] + projected
    if part != ORDER[-1]:
        refs[-2][...] = projected
        refs[-1][...] = chunk_gram(chunk_ref, n)
        return
    kept_ref, sent_ref, projected_ref = refs[-3:]
    half = kept_ref.shape[1]
    projected_ref[...] = projected
    kept_ref[...] = projected_ref[:, pl.ds(pl.multiple_of(core() * half, half), half)]
    sent_ref[...] = projected_ref[:, pl.ds(pl.multiple_of((1 - core()) * half, half), half)]


def gram_kernel(chunk_ref, *refs):
    *refs, out_ref = refs
    n = out_ref.shape[0]
    parts = {part: ref[...] for part, ref in zip(ORDER, refs)}
    parts[ORDER[-1]] = chunk_gram(chunk_ref, n)
    out_ref[...] = jnp.zeros(out_ref.shape, F32)
    out_ref[:, :n] = (parts[0] + parts[1]) + (parts[2] + parts[3])


def inverse_factor_kernel(own_ref, got_ref, out_ref):
    n = own_ref.shape[0]
    gram = (own_ref[...] + got_ref[...])[:, :n]
    work = jnp.concatenate([gram, diagonal(n).astype(F32)], axis=1)
    index = lax.broadcasted_iota(jnp.int32, (n, 1), 0)
    scale = jnp.zeros((n, 1), F32)
    for k in range(n):
        pivot = work[k : k + 1, k : k + 1]
        factor = jnp.where(index > k, work[:, k : k + 1] / pivot, 0.0)
        scale = jnp.where(index == k, lax.rsqrt(pivot), scale)
        work = work - factor * work[k : k + 1, :]
    out_ref[...] = work[:, n:] * scale


def first_term(weights, rows, counts, centre, out_ref):
    n, width = counts.shape[0], out_ref.shape[1]
    term = jnp.dot(weights, rows, preferred_element_type=F32)
    sums = term[2 * n : 2 * n + 1]
    out_ref[:n, :] = join(term[: 2 * n]) + centre * sums
    out_ref[n:, :] = jnp.zeros((EXTRA, width), F32)
    out_ref[n : n + 1, :] = sums
    counts = jnp.where(diagonal(n), counts, 0.0)
    out_ref[n + 1 : n + 2, :n] = jnp.sum(counts, axis=0, keepdims=True)


def first_image_kernel(own_ref, got_ref, rows_ref, *outs):
    *outs, weights_ref, side_ref = outs
    tokens, n, width = rows_ref.shape[0], own_ref.shape[0], outs[0].shape[1]
    projected = total(own_ref, got_ref)[:, :tokens]
    centre = [jnp.sum(ref[:, tokens:].astype(F32), axis=1, keepdims=True) for ref in (own_ref, got_ref)]
    centre = centre[0] + centre[1]
    weights = split(projected)
    counts = join(jnp.sum(weights.astype(F32), axis=1, keepdims=True)) + centre * tokens
    weights = jnp.concatenate([weights, jnp.ones((2 * EXTRA, tokens), BF16)], axis=0)
    for part, out in zip(ORDER[1:], outs):
        place = pl.ds(pl.multiple_of((position() ^ part) * width, width), width)
        first_term(weights, rows_ref[:, place], counts, centre, out)
    weights_ref[...] = weights
    side_ref[...] = jnp.broadcast_to(counts, side_ref.shape)
    side_ref[:, 1:2] = centre


def first_own_image_kernel(weights_ref, side_ref, rows_ref, out_ref):
    width = out_ref.shape[1]
    place = pl.ds(pl.multiple_of(position() * width, width), width)
    first_term(weights_ref[...], rows_ref[:, place], side_ref[:, :1], side_ref[:, 1:2], out_ref)


def first_total_kernel(rows_in_all, own_ref, got_ref, out_ref):
    n = own_ref.shape[0] - EXTRA
    value = own_ref[...] + got_ref[...]
    mean = value[n : n + 1] / rows_in_all
    counts = jnp.where(diagonal(n), value[n + 1 : n + 2, :n], 0.0)
    counts = jnp.sum(counts, axis=1, keepdims=True)
    out_ref[:n, :] = value[:n] - counts * mean
    out_ref[n:, :] = jnp.broadcast_to(mean, (EXTRA, mean.shape[1]))


def gather_halves(own_ref, other_ref, projected_ref):
    half = own_ref.shape[1]
    for place, ref in ((core(), own_ref), (1 - core(), other_ref)):
        projected_ref[:, pl.ds(pl.multiple_of(place * half, half), half)] = ref[...]
    return projected_ref[...]


def image_kernel(own_ref, other_ref, rows_ref, *refs):
    means, outs = refs[: PEERS - 1], refs[PEERS - 1 : -3]
    weights_ref, side_ref, projected_ref = refs[-3:]
    n, width = own_ref.shape[0], outs[0].shape[1]
    weights = split(gather_halves(own_ref, other_ref, projected_ref), TERMS)
    counts = join(jnp.sum(weights.astype(F32), axis=1, keepdims=True), TERMS)
    for part, mean, out in zip(ORDER[1:], means, outs):
        place = pl.ds(pl.multiple_of((position() ^ part) * width, width), width)
        term = join(jnp.dot(weights, rows_ref[:, place], preferred_element_type=F32), TERMS)
        out[...] = term - counts * mean[n : n + 1, :]
    weights_ref[...] = weights
    side_ref[...] = jnp.broadcast_to(counts, side_ref.shape)


def own_image_kernel(weights_ref, side_ref, rows_ref, mean_ref, out_ref):
    n, width = out_ref.shape
    place = pl.ds(pl.multiple_of(position() * width, width), width)
    term = join(jnp.dot(weights_ref[...], rows_ref[:, place], preferred_element_type=F32), TERMS)
    out_ref[...] = term - side_ref[:, :1] * mean_ref[n : n + 1, :]


def assemble_kernel(*refs):
    *chunks, out_ref = refs
    n, width = out_ref.shape[0], chunks[0].shape[1]
    for part, chunk in zip(ORDER, chunks):
        place = pl.ds(pl.multiple_of((position() ^ part) * width, width), width)
        out_ref[:, place] = chunk[:n, :]


def last_kernel(own_ref, other_ref, lower_ref, image_ref, scores_ref, basis_ref, projected_ref):
    n, lower = own_ref.shape[0], lower_ref[...]
    basis_ref[...] = jnp.dot(lower, image_ref[...], preferred_element_type=F32, precision=HIGHEST)
    projected = gather_halves(own_ref, other_ref, projected_ref)
    projected = jnp.dot(lower, projected, preferred_element_type=F32, precision=HIGHEST)
    scores_ref[...] = jnp.sum(projected * projected, axis=0) / n


def normalised_total_kernel(own_ref, got_ref, lower_ref, out_ref):
    value = own_ref[...] + got_ref[...]
    out_ref[...] = jnp.dot(lower_ref[...], value, preferred_element_type=F32, precision=HIGHEST)


def add_kernel(*refs):
    refs[-1][...] = total(*refs[:-1]).astype(refs[-1].dtype)


def add(*terms, dtype=F32):
    return call(add_kernel, [(terms[0].shape, dtype)], "add")(*terms)[0]


def first_part_kernel(*refs):
    *terms, out_ref = refs
    tokens = out_ref.shape[1] - LANES
    value = total(*terms)
    centre = jnp.sum(value, axis=1, keepdims=True) / tokens
    out_ref[:, :tokens] = (value - centre).astype(BF16)
    out_ref[:, tokens:] = jnp.zeros((value.shape[0], LANES), BF16)
    for lane in range(3):
        term = centre.astype(BF16)
        out_ref[:, tokens + lane : tokens + lane + 1] = term
        centre = centre - term.astype(F32)


def swap(value, axis, distance):
    size = lax.axis_size(axis)
    return lax.ppermute(value, axis, [(i, i ^ distance) for i in range(size)])


def distances(axis, start):
    step, size = start, lax.axis_size(axis)
    while step < size:
        yield step
        step *= 2


def sum_but_last(value, axis):
    terms = [value]
    for step in list(distances(axis, 1))[:-1]:
        terms = [add(*terms)] if len(terms) > 1 else terms
        terms.append(swap(terms[0], axis, step))
    return terms


def share(value, axis):
    return [value] + [swap(value, axis, part) for part in ORDER[1:]]


def on_device(activations, start_basis):
    tokens, features = activations.shape
    n = start_basis.shape[0]
    width = features // PEERS
    rows_in_all = tokens * lax.axis_size("tok")
    last_feat = lax.axis_size("feat") // 2

    blocks = 3
    partial, rows = call(
        functools.partial(first_projection_kernel, blocks),
        [((n, tokens), F32), (activations.shape, BF16)],
        "first_projection",
        scratch=[pltpu.VMEM((n, features), F32), pltpu.SemaphoreType.DMA((blocks + 1,))],
        in_specs=[HBM, HBM],
        mebibytes=46,
    )(start_basis, activations)
    terms = sum_but_last(partial, "feat")
    own = call(first_part_kernel, [((n, tokens + LANES), BF16)], "first_part")(*terms)[0]
    got = swap(own, "feat", last_feat)
    side = ((n, LANES), F32)
    half = ((n, tokens // 2), F32)
    whole = ((n, tokens), F32)
    for step in range(ITERS):
        first = step == 0
        chunk = ((n + EXTRA if first else n, width), F32)
        weights = ((2 * n + 2 * EXTRA if first else TERMS * n, tokens), BF16)
        outputs = [chunk] * (PEERS - 1) + [weights, side]
        if first:
            *terms, weights, sums = call(first_image_kernel, outputs, "first_image")(own, got, rows)
            kernel, kept_means = first_own_image_kernel, []
        else:
            kernel, kept_means = own_image_kernel, means[:1]
            scratch = [pltpu.VMEM(*whole)]
            *terms, weights, sums = call(image_kernel, outputs, "image", scratch)(
                own, other, rows, *means[1:]
            )
        received = [swap(term, "tok", part) for part, term in zip(ORDER[1:], terms)]
        kept = call(kernel, [chunk], "own_image", cost=SHORT)(weights, sums, rows, *kept_means)
        image = add(*kept, *received)
        *steps, last_step = distances("tok", PEERS)
        for distance in steps:
            image = add(image, swap(image, "tok", distance))
        kernel = functools.partial(first_total_kernel, rows_in_all) if first else normalised_total_kernel
        lower = [] if first else [lower]
        image = call(kernel, [chunk], "total")(image, swap(image, "tok", last_step), *lower)[0]
        images = share(image, "tok")
        if first:
            means = images
        before, grams = [], []
        for place, part in enumerate(ORDER):
            kernel = functools.partial(projection_kernel, part, first)
            operands = [images[place], rows, *([] if first else [means[place]]), *before]
            if part != ORDER[-1]:
                outputs = [whole, ((n, n), F32)]
                *before, gram = call(kernel, outputs, "projection", cost=SHORT)(*operands)
                grams.append(gram)
        gram = call(gram_kernel, [side], "gram")(images[-1], *grams)[0]
        outputs, scratch = [half, half], [pltpu.VMEM(*whole)]
        own, sent = call(kernel, outputs, "last_projection", scratch, cost=SHORT)(*operands)
        for distance in distances("feat", 1):
            got = swap(sent if distance == 1 else own, "feat", distance)
            narrow = step == ITERS - 1 and distance != last_feat
            own = add(own, got, dtype=BF16 if narrow else F32)
            grams = (gram, swap(gram, "feat", distance))
            gram = add(*grams) if distance != last_feat else None
        other = swap(own, "feat", 1)
        lower = call(inverse_factor_kernel, [((n, n), F32)], "inverse_factor", cost=LONG)(*grams)[0]
    image = call(assemble_kernel, [((n, features), F32)], "assemble")(*images)[0]
    outputs, scratch = [((tokens,), F32), ((n, features), F32)], [pltpu.VMEM(*whole)]
    return tuple(call(last_kernel, outputs, "last", scratch)(own, other, lower, image))


def solution(mesh):
    in_specs = (P("tok", "feat"), P(None, "feat"))
    out_specs = (P("tok"), P(None, "feat"))
    return jax.shard_map(
        on_device, mesh=mesh, in_specs=in_specs, out_specs=out_specs, check_vma=False
    )
```

```python
import functools

import jax
import jax.numpy as jnp
from jax import lax
from jax.experimental import pallas as pl
from jax.experimental.pallas import tpu as pltpu
from jax.sharding import PartitionSpec as P

ITERS = 4
PEERS = 4
LANES = 128
EXTRA = 8
ORDER = (0, 3, 1, 2)
TERMS = 3
LONG = pl.CostEstimate(flops=2**34, bytes_accessed=0, transcendentals=0)
SHORT = pl.CostEstimate(flops=2**29, bytes_accessed=0, transcendentals=0)
HIGHEST = lax.Precision.HIGHEST
VMEM = pl.BlockSpec(memory_space=pltpu.VMEM)
HBM = pl.BlockSpec(memory_space=pltpu.HBM)
F32 = jnp.float32
BF16 = jnp.bfloat16


def call(kernel, outputs, name, scratch=(), in_specs=None, aliases=None, mebibytes=20, cost=None):
    def run(*args):
        specs = in_specs or [VMEM] * len(args)
        return pl.pallas_call(
            kernel,
            out_shape=[jax.ShapeDtypeStruct(shape, dtype) for shape, dtype in outputs],
            in_specs=specs,
            out_specs=[VMEM] * len(outputs),
            scratch_shapes=scratch,
            compiler_params=pltpu.CompilerParams(vmem_limit_bytes=mebibytes * 2**20),
            cost_estimate=cost,
            input_output_aliases=aliases or {},
            name=name,
        )(*args)

    return run


def split(value, terms=2):
    parts = []
    for _ in range(terms):
        parts.append(value.astype(BF16))
        value = value - parts[-1].astype(F32)
    return jnp.concatenate(parts, axis=0)


def join(value, terms=2):
    height = value.shape[0] // terms
    result = value[-height:]
    for term in range(terms - 2, -1, -1):
        result = value[term * height : (term + 1) * height] + result
    return result


def total(*refs):
    terms = [ref[...].astype(F32) for ref in refs]
    while len(terms) > 1:
        terms = [sum(terms[i + 1 : i + 2], terms[i]) for i in range(0, len(terms), 2)]
    return terms[0]


def contract_last(left, right, precision=None):
    return lax.dot_general(
        left, right, (((1,), (1,)), ((), ())), preferred_element_type=F32, precision=precision
    )


def position():
    return lax.rem(lax.axis_index("tok"), PEERS)


def diagonal(n):
    return lax.broadcasted_iota(jnp.int32, (n, n), 0) == lax.broadcasted_iota(jnp.int32, (n, n), 1)


def row_blocks(first, last, sizes):
    starts = [first]
    for size in sizes:
        starts.append(starts[-1] + size)
    return [pl.ds(start, size) for start, size in zip(starts, sizes)]


def fetch(rows_hbm, rows_ref, places, sems):
    copies = [
        pltpu.make_async_copy(rows_hbm.at[place, :], rows_ref.at[place, :], sems.at[i])
        for i, place in enumerate(places)
    ]
    for copy in copies:
        copy.start()
    return copies


def fetch_kernel(places, rows_hbm, rows_ref, sems):
    for copy in fetch(rows_hbm, rows_ref, places, sems):
        copy.wait()


def first_projection_kernel(ready, places, basis_ref, rows_hbm, ready_ref, out_ref, rows_ref, sems):
    copies = fetch(rows_hbm, rows_ref, places, sems)
    vectors = split(basis_ref[...])
    for place in ready:
        out_ref[:, place] = join(contract_last(vectors, rows_ref[place, :]))
    for copy, place in zip(copies, places):
        copy.wait()
        out_ref[:, place] = join(contract_last(vectors, rows_ref[place, :]))


def core():
    return lax.rem(lax.axis_index("feat"), 2)


def aligned(index, size):
    return pl.ds(pl.multiple_of(index * size, size), size)


def chunk_projection(part, chunk_ref, mean_ref, rows_ref, tokens):
    n, width = mean_ref.shape[0] - EXTRA, chunk_ref.shape[1]
    chunk = chunk_ref[:n, :]
    shift = jnp.sum(chunk * mean_ref[n : n + 1, :], axis=1, keepdims=True)
    rows = rows_ref[tokens, aligned(position() ^ part, width)]
    return join(contract_last(split(chunk), rows)) - shift


def own_projection_kernel(chunk_ref, mean_ref, rows_ref, out_ref):
    out_ref[...] = chunk_projection(0, chunk_ref, mean_ref, rows_ref, slice(None))


def rest_projection_kernel(kept, *refs):
    chunks, means, (rows_ref, own_ref), out_ref = refs[:3], refs[3:6], refs[6:8], refs[-1]
    place = aligned(core() if kept else 1 - core(), out_ref.shape[1])
    value = own_ref[:, place]
    for part, chunk_ref, mean_ref in zip(ORDER[1:], chunks, means):
        value = value + chunk_projection(part, chunk_ref, mean_ref, rows_ref, place)
    out_ref[...] = value


def gram_kernel(*refs):
    *refs, out_ref = refs
    n = out_ref.shape[0]
    chunks = {part: ref[:n, :] for part, ref in zip(ORDER, refs)}
    parts = [contract_last(chunks[part], chunks[part], HIGHEST) for part in range(PEERS)]
    out_ref[...] = jnp.zeros(out_ref.shape, F32)
    out_ref[:, :n] = (parts[0] + parts[1]) + (parts[2] + parts[3])


def inverse_factor_kernel(own_ref, got_ref, out_ref):
    n = own_ref.shape[0]
    gram = (own_ref[...] + got_ref[...])[:, :n]
    work = jnp.concatenate([gram, diagonal(n).astype(F32)], axis=1)
    index = lax.broadcasted_iota(jnp.int32, (n, 1), 0)
    scale = jnp.zeros((n, 1), F32)
    for k in range(n):
        pivot = work[k : k + 1, k : k + 1]
        factor = jnp.where(index > k, work[:, k : k + 1] / pivot, 0.0)
        scale = jnp.where(index == k, lax.rsqrt(pivot), scale)
        work = work - factor * work[k : k + 1, :]
    out_ref[...] = work[:, n:] * scale


def first_term(weights, rows, counts, centre, out_ref):
    n, width = counts.shape[0], out_ref.shape[1]
    term = jnp.dot(weights, rows, preferred_element_type=F32)
    sums = term[2 * n : 2 * n + 1]
    out_ref[:n, :] = join(term[: 2 * n]) + centre * sums
    out_ref[n:, :] = jnp.zeros((EXTRA, width), F32)
    out_ref[n : n + 1, :] = sums
    counts = jnp.where(diagonal(n), counts, 0.0)
    out_ref[n + 1 : n + 2, :n] = jnp.sum(counts, axis=0, keepdims=True)


def first_image_kernel(own_ref, got_ref, rows_ref, *outs):
    *outs, weights_ref, side_ref = outs
    tokens, n, width = rows_ref.shape[0], own_ref.shape[0], outs[0].shape[1]
    projected = total(own_ref, got_ref)[:, :tokens]
    centre = [jnp.sum(ref[:, tokens:].astype(F32), axis=1, keepdims=True) for ref in (own_ref, got_ref)]
    centre = centre[0] + centre[1]
    weights = split(projected)
    counts = join(jnp.sum(weights.astype(F32), axis=1, keepdims=True)) + centre * tokens
    weights = jnp.concatenate([weights, jnp.ones((2 * EXTRA, tokens), BF16)], axis=0)
    for part, out in zip(ORDER[1:], outs):
        place = aligned(position() ^ part, width)
        first_term(weights, rows_ref[:, place], counts, centre, out)
    weights_ref[...] = weights
    side_ref[...] = jnp.broadcast_to(counts, side_ref.shape)
    side_ref[:, 1:2] = centre


def first_own_image_kernel(weights_ref, side_ref, rows_ref, out_ref):
    width = out_ref.shape[1]
    place = aligned(position(), width)
    first_term(weights_ref[...], rows_ref[:, place], side_ref[:, :1], side_ref[:, 1:2], out_ref)


def first_total_kernel(rows_in_all, own_ref, got_ref, out_ref):
    n = own_ref.shape[0] - EXTRA
    value = own_ref[...] + got_ref[...]
    mean = value[n : n + 1] / rows_in_all
    counts = jnp.where(diagonal(n), value[n + 1 : n + 2, :n], 0.0)
    counts = jnp.sum(counts, axis=1, keepdims=True)
    out_ref[:n, :] = value[:n] - counts * mean
    out_ref[n:, :] = jnp.broadcast_to(mean, (EXTRA, mean.shape[1]))


def gather_halves(own_ref, other_ref, projected_ref):
    half = own_ref.shape[1]
    for place, ref in ((core(), own_ref), (1 - core(), other_ref)):
        projected_ref[:, pl.ds(pl.multiple_of(place * half, half), half)] = ref[...]
    return projected_ref[...]


def weights_of(projected_ref):
    weights = split(projected_ref[...], TERMS)
    return weights, join(jnp.sum(weights.astype(F32), axis=1, keepdims=True), TERMS)


def image_term(weights, counts, rows, mean_ref):
    n = counts.shape[0]
    term = join(jnp.dot(weights, rows, preferred_element_type=F32), TERMS)
    return term - counts * mean_ref[n : n + 1, :]


def half_image_kernel(own_ref, rows_ref, *refs):
    means, outs = refs[:PEERS], refs[PEERS:]
    tokens = aligned(core(), own_ref.shape[1])
    weights, counts = weights_of(own_ref)
    for part, mean_ref, out_ref in zip(ORDER, means, outs):
        rows = rows_ref[tokens, aligned(position() ^ part, out_ref.shape[1])]
        out_ref[...] = image_term(weights, counts, rows, mean_ref)


def image_kernel(other_ref, rows_ref, *refs):
    means, halves, outs = refs[: PEERS - 1], refs[PEERS - 1 : 2 * PEERS - 2], refs[2 * PEERS - 2 :]
    *outs, weights_ref, side_ref = outs
    tokens = aligned(1 - core(), other_ref.shape[1])
    weights, counts = weights_of(other_ref)
    for part, mean_ref, half_ref, out_ref in zip(ORDER[1:], means, halves, outs):
        rows = rows_ref[tokens, aligned(position() ^ part, out_ref.shape[1])]
        out_ref[...] = half_ref[...] + image_term(weights, counts, rows, mean_ref)
    weights_ref[...] = weights
    side_ref[...] = jnp.broadcast_to(counts, side_ref.shape)


def own_image_kernel(weights_ref, side_ref, rows_ref, mean_ref, half_ref, out_ref):
    tokens = aligned(1 - core(), weights_ref.shape[1])
    rows = rows_ref[tokens, aligned(position(), out_ref.shape[1])]
    out_ref[...] = half_ref[...] + image_term(weights_ref[...], side_ref[:, :1], rows, mean_ref)


def gather_halves(own_ref, other_ref, projected_ref):
    half = own_ref.shape[1]
    projected_ref[:, aligned(core(), half)] = own_ref[...]
    projected_ref[:, aligned(1 - core(), half)] = other_ref[...]
    return projected_ref[...]


def assemble_kernel(*refs):
    *chunks, out_ref = refs
    n, width = out_ref.shape[0], chunks[0].shape[1]
    for part, chunk in zip(ORDER, chunks):
        place = aligned(position() ^ part, width)
        out_ref[:, place] = chunk[:n, :]


def last_kernel(own_ref, other_ref, lower_ref, image_ref, scores_ref, basis_ref, projected_ref):
    n, lower = own_ref.shape[0], lower_ref[...]
    basis_ref[...] = jnp.dot(lower, image_ref[...], preferred_element_type=F32, precision=HIGHEST)
    projected = gather_halves(own_ref, other_ref, projected_ref)
    projected = jnp.dot(lower, projected, preferred_element_type=F32, precision=HIGHEST)
    scores_ref[...] = jnp.sum(projected * projected, axis=0) / n


def normalised_total_kernel(own_ref, got_ref, lower_ref, out_ref):
    value = own_ref[...] + got_ref[...]
    out_ref[...] = jnp.dot(lower_ref[...], value, preferred_element_type=F32, precision=HIGHEST)


def ordered_add_kernel(own_ref, got_ref, before_ref, out_ref):
    out_ref[...] = total(own_ref, got_ref).astype(out_ref.dtype)


def add_kernel(*refs):
    refs[-1][...] = total(*refs[:-1]).astype(refs[-1].dtype)


def add(*terms, dtype=F32):
    return call(add_kernel, [(terms[0].shape, dtype)], "add")(*terms)[0]


def first_part_kernel(*refs):
    *terms, out_ref = refs
    tokens = out_ref.shape[1] - LANES
    value = total(*terms)
    centre = jnp.sum(value, axis=1, keepdims=True) / tokens
    out_ref[:, :tokens] = (value - centre).astype(BF16)
    out_ref[:, tokens:] = jnp.zeros((value.shape[0], LANES), BF16)
    for lane in range(3):
        term = centre.astype(BF16)
        out_ref[:, tokens + lane : tokens + lane + 1] = term
        centre = centre - term.astype(F32)


def swap(value, axis, distance):
    size = lax.axis_size(axis)
    return lax.ppermute(value, axis, [(i, i ^ distance) for i in range(size)])


def distances(axis, start):
    step, size = start, lax.axis_size(axis)
    while step < size:
        yield step
        step *= 2


def sum_but_last(value, axis):
    terms = [value]
    for step in list(distances(axis, 1))[:-1]:
        terms = [add(*terms)] if len(terms) > 1 else terms
        terms.append(swap(terms[0], axis, step))
    return terms


def share(value, axis):
    return [value] + [swap(value, axis, part) for part in ORDER[1:]]


def on_device(activations, start_basis):
    tokens, features = activations.shape
    n = start_basis.shape[0]
    width = features // PEERS
    rows_in_all = tokens * lax.axis_size("tok")
    last_feat = lax.axis_size("feat") // 2

    ready = row_blocks(0, tokens, [tokens // 2])
    places = row_blocks(tokens // 2, tokens, [tokens // 3, tokens // 6])
    rows = call(
        functools.partial(fetch_kernel, ready),
        [(activations.shape, BF16)],
        "fetch",
        scratch=[pltpu.SemaphoreType.DMA((len(ready),))],
        in_specs=[HBM],
        mebibytes=46,
    )(activations)[0]
    partial, rows = call(
        functools.partial(first_projection_kernel, ready, places),
        [((n, tokens), F32), (activations.shape, BF16)],
        "first_projection",
        scratch=[pltpu.SemaphoreType.DMA((len(places),))],
        in_specs=[VMEM, HBM, VMEM],
        aliases={2: 1},
        mebibytes=46,
    )(start_basis, activations, rows)
    terms = sum_but_last(partial, "feat")
    own = call(first_part_kernel, [((n, tokens + LANES), BF16)], "first_part")(*terms)[0]
    got = swap(own, "feat", last_feat)
    side = ((n, LANES), F32)
    half = ((n, tokens // 2), F32)
    whole = ((n, tokens), F32)
    for step in range(ITERS):
        first = step == 0
        chunk = ((n + EXTRA if first else n, width), F32)
        if first:
            weights = ((2 * n + 2 * EXTRA, tokens), BF16)
            outputs = [chunk] * (PEERS - 1) + [weights, side]
            *terms, weights, sums = call(first_image_kernel, outputs, "first_image")(own, got, rows)
            kernel, kept = first_own_image_kernel, []
        else:
            weights = ((TERMS * n, tokens // 2), BF16)
            halves = call(half_image_kernel, [chunk] * PEERS, "half_image", cost=SHORT)(own, rows, *means)
            outputs = [chunk] * (PEERS - 1) + [weights, side]
            *terms, weights, sums = call(image_kernel, outputs, "image")(
                other, rows, *means[1:], *halves[1:]
            )
            kernel, kept = own_image_kernel, [means[0], halves[0]]
        received = [swap(term, "tok", part) for part, term in zip(ORDER[1:], terms)]
        kept = call(kernel, [chunk], "own_image", cost=SHORT)(weights, sums, rows, *kept)
        image = add(*kept, *received)
        *steps, last_step = distances("tok", PEERS)
        for distance in steps:
            image = add(image, swap(image, "tok", distance))
        kernel = functools.partial(first_total_kernel, rows_in_all) if first else normalised_total_kernel
        lower = [] if first else [lower]
        image = call(kernel, [chunk], "total")(image, swap(image, "tok", last_step), *lower)[0]
        images = share(image, "tok")
        if first:
            means = images
        last = step == ITERS - 1
        projected = call(own_projection_kernel, [whole], "own_projection", cost=SHORT)(
            images[0], means[0], rows
        )[0]
        gram = call(gram_kernel, [side], "gram")(*images)[0]
        operands = [*images[1:], *means[1:], rows, projected]
        kernel = functools.partial(rest_projection_kernel, False)
        sent = call(kernel, [half], "sent_projection")(*operands, *([gram] if last else []))[0]
        kernel = functools.partial(rest_projection_kernel, True)
        own = call(kernel, [half], "kept_projection", cost=SHORT)(*operands)[0]
        for distance in distances("feat", 1):
            grams = (gram, swap(gram, "feat", distance))
            gram = add(*grams) if distance != last_feat else None
            got = swap(sent if distance == 1 else own, "feat", distance)
            if last and distance == 1:
                own = call(ordered_add_kernel, [(half[0], BF16)], "add")(own, got, gram)[0]
            elif distance == last_feat:
                own = call(ordered_add_kernel, [half], "add")(own, got, grams[0])[0]
            else:
                own = add(own, got)
        other = swap(own, "feat", 1)
        lower = call(inverse_factor_kernel, [((n, n), F32)], "inverse_factor", cost=LONG)(*grams)[0]
    image = call(assemble_kernel, [((n, features), F32)], "assemble")(*images)[0]
    outputs, scratch = [((tokens,), F32), ((n, features), F32)], [pltpu.VMEM(*whole)]
    return tuple(call(last_kernel, outputs, "last", scratch)(own, other, lower, image))


def solution(mesh):
    in_specs = (P("tok", "feat"), P(None, "feat"))
    out_specs = (P("tok"), P(None, "feat"))
    return jax.shard_map(
        on_device, mesh=mesh, in_specs=in_specs, out_specs=out_specs, check_vma=False
    )
```

```python
import functools

import jax
import jax.numpy as jnp
from jax import lax
from jax.experimental import pallas as pl
from jax.experimental.pallas import tpu as pltpu
from jax.sharding import PartitionSpec as P

ITERS = 4
PEERS = 4
LANES = 128
EXTRA = 8
ORDER = (0, 3, 1, 2)
TERMS = 3
LONG = pl.CostEstimate(flops=2**34, bytes_accessed=0, transcendentals=0)
SHORT = pl.CostEstimate(flops=2**29, bytes_accessed=0, transcendentals=0)
HIGHEST = lax.Precision.HIGHEST
VMEM = pl.BlockSpec(memory_space=pltpu.VMEM)
HBM = pl.BlockSpec(memory_space=pltpu.HBM)
F32 = jnp.float32
BF16 = jnp.bfloat16


def call(kernel, outputs, name, scratch=(), in_specs=None, aliases=None, mebibytes=20, cost=None):
    def run(*args):
        specs = in_specs or [VMEM] * len(args)
        return pl.pallas_call(
            kernel,
            out_shape=[jax.ShapeDtypeStruct(shape, dtype) for shape, dtype in outputs],
            in_specs=specs,
            out_specs=[VMEM] * len(outputs),
            scratch_shapes=scratch,
            compiler_params=pltpu.CompilerParams(vmem_limit_bytes=mebibytes * 2**20),
            cost_estimate=cost,
            input_output_aliases=aliases or {},
            name=name,
        )(*args)

    return run


def split(value, terms=2):
    parts = []
    for _ in range(terms):
        parts.append(value.astype(BF16))
        value = value - parts[-1].astype(F32)
    return jnp.concatenate(parts, axis=0)


def join(value, terms=2):
    height = value.shape[0] // terms
    result = value[-height:]
    for term in range(terms - 2, -1, -1):
        result = value[term * height : (term + 1) * height] + result
    return result


def total(*refs):
    terms = [ref[...].astype(F32) for ref in refs]
    while len(terms) > 1:
        terms = [sum(terms[i + 1 : i + 2], terms[i]) for i in range(0, len(terms), 2)]
    return terms[0]


def contract_last(left, right, precision=None):
    return lax.dot_general(
        left, right, (((1,), (1,)), ((), ())), preferred_element_type=F32, precision=precision
    )


def position():
    return lax.rem(lax.axis_index("tok"), PEERS)


def diagonal(n):
    return lax.broadcasted_iota(jnp.int32, (n, n), 0) == lax.broadcasted_iota(jnp.int32, (n, n), 1)


def row_blocks(first, last, sizes):
    starts = [first]
    for size in sizes:
        starts.append(starts[-1] + size)
    return [pl.ds(start, size) for start, size in zip(starts, sizes)]


def fetch(rows_hbm, rows_ref, places, sems):
    copies = [
        pltpu.make_async_copy(rows_hbm.at[place, :], rows_ref.at[place, :], sems.at[i])
        for i, place in enumerate(places)
    ]
    for copy in copies:
        copy.start()
    return copies


def fetch_kernel(places, rows_hbm, rows_ref, sems):
    for copy in fetch(rows_hbm, rows_ref, places, sems):
        copy.wait()


def first_projection_kernel(ready, places, basis_ref, rows_hbm, ready_ref, out_ref, rows_ref, sems):
    copies = fetch(rows_hbm, rows_ref, places, sems)
    vectors = split(basis_ref[...])
    for place in ready:
        out_ref[:, place] = join(contract_last(vectors, rows_ref[place, :]))
    for copy, place in zip(copies, places):
        copy.wait()
        out_ref[:, place] = join(contract_last(vectors, rows_ref[place, :]))


def core():
    return lax.rem(lax.axis_index("feat"), 2)


def aligned(index, size):
    return pl.ds(pl.multiple_of(index * size, size), size)


def split_kernel(chunk_ref, out_ref):
    out_ref[...] = split(chunk_ref[: out_ref.shape[0] // 2, :])


def chunk_projection(part, terms, chunk_ref, mean_ref, rows_ref, tokens):
    n, width = mean_ref.shape[0] - EXTRA, chunk_ref.shape[1]
    shift = jnp.sum(chunk_ref[:n, :] * mean_ref[n : n + 1, :], axis=1, keepdims=True)
    rows = rows_ref[tokens, aligned(position() ^ part, width)]
    return join(contract_last(terms, rows)) - shift


def own_projection_kernel(chunk_ref, mean_ref, rows_ref, out_ref):
    terms = split(chunk_ref[: out_ref.shape[0], :])
    out_ref[...] = chunk_projection(0, terms, chunk_ref, mean_ref, rows_ref, slice(None))


def rest_projection_kernel(half, chunk3, chunk1, chunk2, mean3, mean1, mean2, terms_ref, rows_ref, own_ref, *refs):
    out_ref = refs[-1]
    n, tokens = out_ref.shape
    place = slice(None) if half is None else aligned(core() if half == "kept" else 1 - core(), tokens)
    value = own_ref[:, place]
    for part, terms, chunk_ref, mean_ref in (
        (3, terms_ref[...], chunk3, mean3),
        (1, split(chunk1[:n, :]), chunk1, mean1),
        (2, split(chunk2[:n, :]), chunk2, mean2),
    ):
        value = value + chunk_projection(part, terms, chunk_ref, mean_ref, rows_ref, place)
    out_ref[...] = value


def gram_kernel(*refs):
    *refs, out_ref = refs
    n = out_ref.shape[0]
    chunks = {part: ref[:n, :] for part, ref in zip(ORDER, refs)}
    parts = [contract_last(chunks[part], chunks[part], HIGHEST) for part in range(PEERS)]
    out_ref[...] = jnp.zeros(out_ref.shape, F32)
    out_ref[:, :n] = (parts[0] + parts[1]) + (parts[2] + parts[3])


def inverse_factor_kernel(own_ref, got_ref, out_ref):
    n = own_ref.shape[0]
    gram = (own_ref[...] + got_ref[...])[:, :n]
    work = jnp.concatenate([gram, diagonal(n).astype(F32)], axis=1)
    index = lax.broadcasted_iota(jnp.int32, (n, 1), 0)
    scale = jnp.zeros((n, 1), F32)
    for k in range(n):
        pivot = work[k : k + 1, k : k + 1]
        factor = jnp.where(index > k, work[:, k : k + 1] / pivot, 0.0)
        scale = jnp.where(index == k, lax.rsqrt(pivot), scale)
        work = work - factor * work[k : k + 1, :]
    out_ref[...] = work[:, n:] * scale


def first_term(weights, rows, counts, centre, out_ref):
    n, width = counts.shape[0], out_ref.shape[1]
    term = jnp.dot(weights, rows, preferred_element_type=F32)
    sums = term[2 * n : 2 * n + 1]
    out_ref[:n, :] = join(term[: 2 * n]) + centre * sums
    out_ref[n:, :] = jnp.zeros((EXTRA, width), F32)
    out_ref[n : n + 1, :] = sums
    counts = jnp.where(diagonal(n), counts, 0.0)
    out_ref[n + 1 : n + 2, :n] = jnp.sum(counts, axis=0, keepdims=True)


def first_image_kernel(own_ref, got_ref, rows_ref, *outs):
    *outs, weights_ref, side_ref = outs
    tokens, n, width = rows_ref.shape[0], own_ref.shape[0], outs[0].shape[1]
    projected = total(own_ref, got_ref)[:, :tokens]
    centre = [jnp.sum(ref[:, tokens:].astype(F32), axis=1, keepdims=True) for ref in (own_ref, got_ref)]
    centre = centre[0] + centre[1]
    weights = split(projected)
    counts = join(jnp.sum(weights.astype(F32), axis=1, keepdims=True)) + centre * tokens
    weights = jnp.concatenate([weights, jnp.ones((2 * EXTRA, tokens), BF16)], axis=0)
    for part, out in zip(ORDER[1:], outs):
        place = aligned(position() ^ part, width)
        first_term(weights, rows_ref[:, place], counts, centre, out)
    weights_ref[...] = weights
    side_ref[...] = jnp.broadcast_to(counts, side_ref.shape)
    side_ref[:, 1:2] = centre


def first_own_image_kernel(weights_ref, side_ref, rows_ref, out_ref):
    width = out_ref.shape[1]
    place = aligned(position(), width)
    first_term(weights_ref[...], rows_ref[:, place], side_ref[:, :1], side_ref[:, 1:2], out_ref)


def first_total_kernel(rows_in_all, own_ref, got_ref, out_ref):
    n = own_ref.shape[0] - EXTRA
    value = own_ref[...] + got_ref[...]
    mean = value[n : n + 1] / rows_in_all
    counts = jnp.where(diagonal(n), value[n + 1 : n + 2, :n], 0.0)
    counts = jnp.sum(counts, axis=1, keepdims=True)
    out_ref[:n, :] = value[:n] - counts * mean
    out_ref[n:, :] = jnp.broadcast_to(mean, (EXTRA, mean.shape[1]))


def weights_of(projected_ref):
    weights = split(projected_ref[...], TERMS)
    return weights, join(jnp.sum(weights.astype(F32), axis=1, keepdims=True), TERMS)


def image_term(weights, counts, rows, mean_ref):
    n = counts.shape[0]
    term = join(jnp.dot(weights, rows, preferred_element_type=F32), TERMS)
    return term - counts * mean_ref[n : n + 1, :]


def half_image_kernel(own_ref, rows_ref, *refs):
    means, outs = refs[:PEERS], refs[PEERS:]
    tokens = aligned(core(), own_ref.shape[1])
    weights, counts = weights_of(own_ref)
    for part, mean_ref, out_ref in zip(ORDER, means, outs):
        rows = rows_ref[tokens, aligned(position() ^ part, out_ref.shape[1])]
        out_ref[...] = image_term(weights, counts, rows, mean_ref)


def image_kernel(other_ref, rows_ref, *refs):
    means, halves, outs = refs[: PEERS - 1], refs[PEERS - 1 : 2 * PEERS - 2], refs[2 * PEERS - 2 :]
    *outs, weights_ref, side_ref = outs
    tokens = aligned(1 - core(), other_ref.shape[1])
    weights, counts = weights_of(other_ref)
    for part, mean_ref, half_ref, out_ref in zip(ORDER[1:], means, halves, outs):
        rows = rows_ref[tokens, aligned(position() ^ part, out_ref.shape[1])]
        out_ref[...] = half_ref[...] + image_term(weights, counts, rows, mean_ref)
    weights_ref[...] = weights
    side_ref[...] = jnp.broadcast_to(counts, side_ref.shape)


def own_image_kernel(weights_ref, side_ref, rows_ref, mean_ref, half_ref, out_ref):
    tokens = aligned(1 - core(), weights_ref.shape[1])
    rows = rows_ref[tokens, aligned(position(), out_ref.shape[1])]
    out_ref[...] = half_ref[...] + image_term(weights_ref[...], side_ref[:, :1], rows, mean_ref)


def assemble_kernel(*refs):
    *chunks, out_ref = refs
    n, width = out_ref.shape[0], chunks[0].shape[1]
    for part, chunk in zip(ORDER, chunks):
        place = aligned(position() ^ part, width)
        out_ref[:, place] = chunk[:n, :]


def last_kernel(own_ref, got_ref, lower_ref, image_ref, scores_ref, basis_ref):
    n, lower = lower_ref.shape[0], lower_ref[...]
    basis_ref[...] = jnp.dot(lower, image_ref[...], preferred_element_type=F32, precision=HIGHEST)
    projected = total(own_ref, got_ref)
    projected = jnp.dot(lower, projected, preferred_element_type=F32, precision=HIGHEST)
    scores_ref[...] = jnp.sum(projected * projected, axis=0) / n


def normalised_total_kernel(own_ref, got_ref, lower_ref, out_ref):
    value = own_ref[...] + got_ref[...]
    out_ref[...] = jnp.dot(lower_ref[...], value, preferred_element_type=F32, precision=HIGHEST)


def ordered_add_kernel(own_ref, got_ref, before_ref, out_ref):
    out_ref[...] = total(own_ref, got_ref).astype(out_ref.dtype)


def add_kernel(*refs):
    refs[-1][...] = total(*refs[:-1]).astype(refs[-1].dtype)


def add(*terms, dtype=F32):
    return call(add_kernel, [(terms[0].shape, dtype)], "add")(*terms)[0]


def first_part_kernel(*refs):
    *terms, out_ref = refs
    tokens = out_ref.shape[1] - LANES
    value = total(*terms)
    centre = jnp.sum(value, axis=1, keepdims=True) / tokens
    out_ref[:, :tokens] = (value - centre).astype(BF16)
    out_ref[:, tokens:] = jnp.zeros((value.shape[0], LANES), BF16)
    for lane in range(3):
        term = centre.astype(BF16)
        out_ref[:, tokens + lane : tokens + lane + 1] = term
        centre = centre - term.astype(F32)


def swap(value, axis, distance):
    size = lax.axis_size(axis)
    return lax.ppermute(value, axis, [(i, i ^ distance) for i in range(size)])


def distances(axis, start):
    step, size = start, lax.axis_size(axis)
    while step < size:
        yield step
        step *= 2


def sum_but_last(value, axis):
    terms = [value]
    for step in list(distances(axis, 1))[:-1]:
        terms = [add(*terms)] if len(terms) > 1 else terms
        terms.append(swap(terms[0], axis, step))
    return terms


def share(value, axis):
    return [value] + [swap(value, axis, part) for part in ORDER[1:]]


def on_device(activations, start_basis):
    tokens, features = activations.shape
    n = start_basis.shape[0]
    width = features // PEERS
    rows_in_all = tokens * lax.axis_size("tok")
    last_feat = lax.axis_size("feat") // 2

    ready = row_blocks(0, tokens, [tokens // 2])
    places = row_blocks(tokens // 2, tokens, [tokens // 3, tokens // 6])
    rows = call(
        functools.partial(fetch_kernel, ready),
        [(activations.shape, BF16)],
        "fetch",
        scratch=[pltpu.SemaphoreType.DMA((len(ready),))],
        in_specs=[HBM],
        mebibytes=46,
    )(activations)[0]
    partial, rows = call(
        functools.partial(first_projection_kernel, ready, places),
        [((n, tokens), F32), (activations.shape, BF16)],
        "first_projection",
        scratch=[pltpu.SemaphoreType.DMA((len(places),))],
        in_specs=[VMEM, HBM, VMEM],
        aliases={2: 1},
        mebibytes=46,
    )(start_basis, activations, rows)
    terms = sum_but_last(partial, "feat")
    own = call(first_part_kernel, [((n, tokens + LANES), BF16)], "first_part")(*terms)[0]
    got = swap(own, "feat", last_feat)
    side = ((n, LANES), F32)
    half = ((n, tokens // 2), F32)
    whole = ((n, tokens), F32)
    for step in range(ITERS):
        first = step == 0
        chunk = ((n + EXTRA if first else n, width), F32)
        if first:
            weights = ((2 * n + 2 * EXTRA, tokens), BF16)
            outputs = [chunk] * (PEERS - 1) + [weights, side]
            *terms, weights, sums = call(first_image_kernel, outputs, "first_image")(own, got, rows)
            kernel, kept = first_own_image_kernel, []
        else:
            weights = ((TERMS * n, tokens // 2), BF16)
            halves = call(half_image_kernel, [chunk] * PEERS, "half_image", cost=SHORT)(own, rows, *means)
            outputs = [chunk] * (PEERS - 1) + [weights, side]
            *terms, weights, sums = call(image_kernel, outputs, "image")(
                other, rows, *means[1:], *halves[1:]
            )
            kernel, kept = own_image_kernel, [means[0], halves[0]]
        received = [swap(term, "tok", part) for part, term in zip(ORDER[1:], terms)]
        kept = call(kernel, [chunk], "own_image", cost=SHORT)(weights, sums, rows, *kept)
        image = add(*kept, *received)
        *steps, last_step = distances("tok", PEERS)
        for distance in steps:
            image = add(image, swap(image, "tok", distance))
        kernel = functools.partial(first_total_kernel, rows_in_all) if first else normalised_total_kernel
        lower = [] if first else [lower]
        image = call(kernel, [chunk], "total")(image, swap(image, "tok", last_step), *lower)[0]
        images = share(image, "tok")
        if first:
            means = images
        last = step == ITERS - 1
        projected = call(own_projection_kernel, [whole], "own_projection", cost=SHORT)(
            images[0], means[0], rows
        )[0]
        terms = call(split_kernel, [((2 * n, width), BF16)], "split", cost=SHORT)(images[1])[0]
        gram = call(gram_kernel, [side], "gram")(*images)[0]
        operands = [*images[1:], *means[1:], terms, rows, projected]
        if last:
            kernel = functools.partial(rest_projection_kernel, None)
            own = call(kernel, [whole], "projection")(*operands, gram)[0]
        else:
            kernel = functools.partial(rest_projection_kernel, "sent")
            sent = call(kernel, [half], "sent_projection")(*operands)[0]
            kernel = functools.partial(rest_projection_kernel, "kept")
            own = call(kernel, [half], "kept_projection", cost=SHORT)(*operands)[0]
        for distance in distances("feat", 1):
            got = swap(own if last or distance > 1 else sent, "feat", distance)
            grams = (gram, swap(gram, "feat", distance))
            gram = add(*grams) if distance != last_feat else None
            if last:
                narrow = ((n, tokens), BF16 if distance == last_feat // 2 else F32)
                if distance != last_feat:
                    own = call(ordered_add_kernel, [narrow], "add")(own, got, gram)[0]
                else:
                    other = got
            elif distance == last_feat:
                own = call(ordered_add_kernel, [half], "add")(own, got, grams[0])[0]
                other = swap(own, "feat", 1)
            else:
                own = add(own, got)
        lower = call(inverse_factor_kernel, [((n, n), F32)], "inverse_factor", cost=LONG)(*grams)[0]
    image = call(assemble_kernel, [((n, features), F32)], "assemble")(*images)[0]
    outputs = [((tokens,), F32), ((n, features), F32)]
    return tuple(call(last_kernel, outputs, "last")(own, other, lower, image))


def solution(mesh):
    in_specs = (P("tok", "feat"), P(None, "feat"))
    out_specs = (P("tok"), P(None, "feat"))
    return jax.shard_map(
        on_device, mesh=mesh, in_specs=in_specs, out_specs=out_specs, check_vma=False
    )
```

```python
import functools

import jax
import jax.numpy as jnp
from jax import lax
from jax.experimental import pallas as pl
from jax.experimental.pallas import tpu as pltpu
from jax.sharding import PartitionSpec as P

ITERS = 4
PEERS = 4
LANES = 128
EXTRA = 8
ORDER = (0, 3, 2, 1)
TERMS = 3
LONG = pl.CostEstimate(flops=2**34, bytes_accessed=0, transcendentals=0)
SHORT = pl.CostEstimate(flops=2**29, bytes_accessed=0, transcendentals=0)
HIGHEST = lax.Precision.HIGHEST
VMEM = pl.BlockSpec(memory_space=pltpu.VMEM)
HBM = pl.BlockSpec(memory_space=pltpu.HBM)
F32 = jnp.float32
BF16 = jnp.bfloat16


def call(kernel, outputs, name, scratch=(), in_specs=None, aliases=None, mebibytes=20, cost=None):
    def run(*args):
        specs = in_specs or [VMEM] * len(args)
        return pl.pallas_call(
            kernel,
            out_shape=[jax.ShapeDtypeStruct(shape, dtype) for shape, dtype in outputs],
            in_specs=specs,
            out_specs=[VMEM] * len(outputs),
            scratch_shapes=scratch,
            compiler_params=pltpu.CompilerParams(vmem_limit_bytes=mebibytes * 2**20),
            cost_estimate=cost,
            input_output_aliases=aliases or {},
            name=name,
        )(*args)

    return run


def split(value, terms=2):
    parts = []
    for _ in range(terms):
        parts.append(value.astype(BF16))
        value = value - parts[-1].astype(F32)
    return jnp.concatenate(parts, axis=0)


def join(value, terms=2):
    height = value.shape[0] // terms
    result = value[-height:]
    for term in range(terms - 2, -1, -1):
        result = value[term * height : (term + 1) * height] + result
    return result


def total(*refs):
    terms = [ref[...].astype(F32) for ref in refs]
    while len(terms) > 1:
        terms = [sum(terms[i + 1 : i + 2], terms[i]) for i in range(0, len(terms), 2)]
    return terms[0]


def contract_last(left, right, precision=None):
    return lax.dot_general(
        left, right, (((1,), (1,)), ((), ())), preferred_element_type=F32, precision=precision
    )


def position():
    return lax.rem(lax.axis_index("tok"), PEERS)


def diagonal(n):
    return lax.broadcasted_iota(jnp.int32, (n, n), 0) == lax.broadcasted_iota(jnp.int32, (n, n), 1)


def core():
    return lax.rem(lax.axis_index("feat"), 2)


def aligned(index, size):
    return pl.ds(pl.multiple_of(index * size, size), size)


def fetch_kernel(rows_hbm, rows_ref, sem):
    place = aligned(1 - core(), rows_ref.shape[0] // 2)
    copy = pltpu.make_async_copy(rows_hbm.at[place, :], rows_ref.at[place, :], sem)
    copy.start()
    copy.wait()


def first_sent_kernel(basis_ref, rows_hbm, ready_ref, out_ref, rows_ref, sem):
    half = out_ref.shape[1]
    place = aligned(core(), half)
    copy = pltpu.make_async_copy(rows_hbm.at[place, :], rows_ref.at[place, :], sem)
    copy.start()
    rows = rows_ref[aligned(1 - core(), half), :]
    out_ref[...] = join(contract_last(split(basis_ref[...]), rows))
    copy.wait()


def first_kept_kernel(basis_ref, rows_ref, out_ref):
    rows = rows_ref[aligned(core(), out_ref.shape[1]), :]
    out_ref[...] = join(contract_last(split(basis_ref[...]), rows))


def projection_kernel(part, half, chunk_ref, mean_ref, rows_ref, *refs):
    out_ref = refs[-1]
    n, tokens = out_ref.shape
    place = {"all": 0, "kept": core(), "sent": 1 - core()}[half]
    place = aligned(place, tokens) if half != "all" else slice(None)
    chunk = chunk_ref[:n, :]
    shift = jnp.sum(chunk * mean_ref[n : n + 1, :], axis=1, keepdims=True)
    rows = rows_ref[place, aligned(position() ^ part, chunk.shape[1])]
    value = join(contract_last(split(chunk), rows)) - shift
    out_ref[...] = value if part == ORDER[0] else refs[0][:, place] + value


def gram_kernel(*refs):
    *refs, out_ref = refs
    n = out_ref.shape[0]
    chunks = {part: ref[:n, :] for part, ref in zip(ORDER, refs)}
    parts = [contract_last(chunks[part], chunks[part], HIGHEST) for part in range(PEERS)]
    out_ref[...] = jnp.zeros(out_ref.shape, F32)
    out_ref[:, :n] = (parts[0] + parts[1]) + (parts[2] + parts[3])


def inverse_factor_kernel(own_ref, got_ref, out_ref):
    n = own_ref.shape[0]
    gram = (own_ref[...] + got_ref[...])[:, :n]
    work = jnp.concatenate([gram, diagonal(n).astype(F32)], axis=1)
    index = lax.broadcasted_iota(jnp.int32, (n, 1), 0)
    scale = jnp.zeros((n, 1), F32)
    for k in range(n):
        pivot = work[k : k + 1, k : k + 1]
        factor = jnp.where(index > k, work[:, k : k + 1] / pivot, 0.0)
        scale = jnp.where(index == k, lax.rsqrt(pivot), scale)
        work = work - factor * work[k : k + 1, :]
    out_ref[...] = work[:, n:] * scale


def first_total_kernel(rows_in_all, own_ref, got_ref, out_ref):
    n = own_ref.shape[0] - EXTRA
    value = own_ref[...] + got_ref[...]
    mean = value[n : n + 1] / rows_in_all
    counts = jnp.where(diagonal(n), value[n + 1 : n + 2, :n], 0.0)
    counts = jnp.sum(counts, axis=1, keepdims=True)
    out_ref[:n, :] = value[:n] - counts * mean
    out_ref[n:, :] = jnp.broadcast_to(mean, (EXTRA, mean.shape[1]))


def weights_of(first, projected_ref):
    projected = projected_ref[...]
    centre = jnp.zeros((projected.shape[0], 1), F32)
    if first:
        centre = jnp.sum(projected, axis=1, keepdims=True) / projected.shape[1]
    weights = split(projected - centre if first else projected, TERMS)
    counts = join(jnp.sum(weights.astype(F32), axis=1, keepdims=True), TERMS)
    if first:
        counts = counts + centre * projected.shape[1]
        weights = jnp.concatenate([weights, jnp.ones((2 * EXTRA, projected.shape[1]), BF16)], axis=0)
    return weights, counts, centre


def image_term(first, weights, counts, centre, rows, mean_ref):
    n = counts.shape[0]
    term = jnp.dot(weights, rows, preferred_element_type=F32)
    value = join(term[: TERMS * n], TERMS)
    if not first:
        return value - counts * mean_ref[n : n + 1, :]
    sums = term[TERMS * n : TERMS * n + 1]
    counts = jnp.sum(jnp.where(diagonal(n), counts, 0.0), axis=0, keepdims=True)
    counts = jnp.concatenate([counts, jnp.zeros((1, sums.shape[1] - n), F32)], axis=1)
    below = jnp.zeros((EXTRA - 2, sums.shape[1]), F32)
    return jnp.concatenate([value + centre * sums, sums, counts, below], axis=0)


def half_image_kernel(first, own_ref, rows_ref, *refs):
    means, outs = ([None] * PEERS if first else refs[:PEERS]), refs[-PEERS:]
    tokens = aligned(core(), own_ref.shape[1])
    sides = weights_of(first, own_ref)
    for part, mean_ref, out_ref in zip(ORDER, means, outs):
        rows = rows_ref[tokens, aligned(position() ^ part, out_ref.shape[1])]
        out_ref[...] = image_term(first, *sides, rows, mean_ref)


def image_kernel(first, other_ref, rows_ref, *refs):
    *refs, weights_ref, side_ref = refs
    peers = PEERS - 1
    means, halves, outs = ([None] * peers if first else refs[:peers]), refs[-2 * peers : -peers], refs[-peers:]
    tokens = aligned(1 - core(), other_ref.shape[1])
    weights, counts, centre = weights_of(first, other_ref)
    for part, mean_ref, half_ref, out_ref in zip(ORDER[1:], means, halves, outs):
        rows = rows_ref[tokens, aligned(position() ^ part, out_ref.shape[1])]
        out_ref[...] = half_ref[...] + image_term(first, weights, counts, centre, rows, mean_ref)
    weights_ref[...] = weights
    side_ref[...] = jnp.broadcast_to(counts, side_ref.shape)
    side_ref[:, 1:2] = centre


def own_image_kernel(first, weights_ref, side_ref, rows_ref, half_ref, *refs):
    mean_ref, out_ref = (None if first else refs[0]), refs[-1]
    tokens = aligned(1 - core(), weights_ref.shape[1])
    rows = rows_ref[tokens, aligned(position(), out_ref.shape[1])]
    sides = weights_ref[...], side_ref[:, :1], side_ref[:, 1:2]
    out_ref[...] = half_ref[...] + image_term(first, *sides, rows, mean_ref)


def assemble_kernel(*refs):
    *chunks, out_ref = refs
    n, width = out_ref.shape[0], chunks[0].shape[1]
    for part, chunk in zip(ORDER, chunks):
        place = aligned(position() ^ part, width)
        out_ref[:, place] = chunk[:n, :]


def last_kernel(own_ref, got_ref, lower_ref, image_ref, scores_ref, basis_ref):
    n, lower = lower_ref.shape[0], lower_ref[...]
    basis_ref[...] = jnp.dot(lower, image_ref[...], preferred_element_type=F32, precision=HIGHEST)
    projected = total(own_ref, got_ref)
    projected = jnp.dot(lower, projected, preferred_element_type=F32, precision=HIGHEST)
    scores_ref[...] = jnp.sum(projected * projected, axis=0) / n


def normalised_total_kernel(own_ref, got_ref, lower_ref, out_ref):
    value = own_ref[...] + got_ref[...]
    out_ref[...] = jnp.dot(lower_ref[...], value, preferred_element_type=F32, precision=HIGHEST)


def ordered_add_kernel(own_ref, got_ref, before_ref, out_ref):
    out_ref[...] = total(own_ref, got_ref).astype(out_ref.dtype)


def add_kernel(*refs):
    refs[-1][...] = total(*refs[:-1]).astype(refs[-1].dtype)


def add(*terms, dtype=F32):
    return call(add_kernel, [(terms[0].shape, dtype)], "add")(*terms)[0]


def swap(value, axis, distance):
    size = lax.axis_size(axis)
    return lax.ppermute(value, axis, [(i, i ^ distance) for i in range(size)])


def distances(axis, start):
    step, size = start, lax.axis_size(axis)
    while step < size:
        yield step
        step *= 2


def share(value, axis):
    return [value] + [swap(value, axis, part) for part in ORDER[1:]]


def on_device(activations, start_basis):
    tokens, features = activations.shape
    n = start_basis.shape[0]
    width = features // PEERS
    rows_in_all = tokens * lax.axis_size("tok")
    last_feat = lax.axis_size("feat") // 2
    side = ((n, LANES), F32)
    half = ((n, tokens // 2), F32)
    whole = ((n, tokens), F32)

    fetched, sem = (activations.shape, BF16), [pltpu.SemaphoreType.DMA(())]
    rows = call(fetch_kernel, [fetched], "fetch", sem, in_specs=[HBM], mebibytes=46)(activations)[0]
    sent, rows = call(
        first_sent_kernel,
        [half, fetched],
        "sent_projection",
        sem,
        in_specs=[VMEM, HBM, VMEM],
        aliases={2: 1},
        mebibytes=46,
    )(start_basis, activations, rows)
    own = call(first_kept_kernel, [half], "kept_projection", cost=SHORT)(start_basis, rows)[0]
    for distance in distances("feat", 1):
        own = add(own, swap(sent if distance == 1 else own, "feat", distance))
    other = swap(own, "feat", 1)
    means, lower = [], []
    for step in range(ITERS):
        first, last = step == 0, step == ITERS - 1
        chunk = ((n + EXTRA if first else n, width), F32)
        weights = ((TERMS * n + 2 * EXTRA if first else TERMS * n, tokens // 2), BF16)
        kernel = functools.partial(half_image_kernel, first)
        kept, *halves = call(kernel, [chunk] * PEERS, "half_image", cost=SHORT)(own, rows, *means)
        kernel = functools.partial(image_kernel, first)
        *terms, weights, sums = call(kernel, [chunk] * (PEERS - 1) + [weights, side], "image")(
            other, rows, *means[1:], *halves
        )
        received = [swap(term, "tok", part) for part, term in zip(ORDER[1:], terms)]
        kernel = functools.partial(own_image_kernel, first)
        kept = call(kernel, [chunk], "own_image", cost=SHORT)(weights, sums, rows, kept, *means[:1])
        image = add(*kept, *received)
        *steps, last_step = distances("tok", PEERS)
        for distance in steps:
            image = add(image, swap(image, "tok", distance))
        kernel = functools.partial(first_total_kernel, rows_in_all) if first else normalised_total_kernel
        image = call(kernel, [chunk], "total")(image, swap(image, "tok", last_step), *lower)[0]
        images = share(image, "tok")
        means = means or images
        gram = call(gram_kernel, [side], "gram")(*images)[0]
        grams = (gram, swap(gram, "feat", 1))
        before = []
        for part, image, mean in zip(ORDER, images, means):
            operands = [image, mean, rows, *before]
            if part != ORDER[-1]:
                kernel = functools.partial(projection_kernel, part, "all")
                before = call(kernel, [whole], "projection", cost=SHORT)(*operands)
        if last:
            gram = add(*grams)
            kernel = functools.partial(projection_kernel, part, "all")
            own = call(kernel, [whole], "projection")(*operands, gram)[0]
            for distance in distances("feat", 1):
                terms = (own, swap(own, "feat", distance))
                if distance != last_feat:
                    narrow = ((n, tokens), BF16 if distance == last_feat // 2 else F32)
                    own = call(add_kernel, [narrow], "add")(*terms)[0]
            own, other = terms
            for distance in distances("feat", 2):
                grams = (gram, swap(gram, "feat", distance))
                gram = add(*grams)
        else:
            kernel = functools.partial(projection_kernel, part, "sent")
            sent = call(kernel, [half], "sent_projection")(*operands)[0]
            kernel = functools.partial(projection_kernel, part, "kept")
            own = call(kernel, [half], "kept_projection", cost=SHORT)(*operands)[0]
            for distance in distances("feat", 1):
                got = swap(sent if distance == 1 else own, "feat", distance)
                if distance > 1:
                    gram = add(*grams)
                    grams = (gram, swap(gram, "feat", distance))
                if distance == last_feat:
                    own = call(ordered_add_kernel, [half], "add")(own, got, gram)[0]
                else:
                    own = add(own, got)
            other = swap(own, "feat", 1)
        lower = call(inverse_factor_kernel, [((n, n), F32)], "inverse_factor", cost=LONG)(*grams)
    image = call(assemble_kernel, [((n, features), F32)], "assemble")(*images)[0]
    outputs = [((tokens,), F32), ((n, features), F32)]
    return tuple(call(last_kernel, outputs, "last")(own, other, *lower, image))


def solution(mesh):
    in_specs = (P("tok", "feat"), P(None, "feat"))
    out_specs = (P("tok"), P(None, "feat"))
    return jax.shard_map(
        on_device, mesh=mesh, in_specs=in_specs, out_specs=out_specs, check_vma=False
    )
```

```python
import functools

import jax
import jax.numpy as jnp
from jax import lax
from jax.experimental import pallas as pl
from jax.experimental.pallas import tpu as pltpu
from jax.sharding import PartitionSpec as P

ITERS = 4
PEERS = 4
LANES = 128
EXTRA = 8
SCATTER = (0, 3, 2, 1)
GATHER = (0, 3, 1, 2)
TERMS = 3
LONG = pl.CostEstimate(flops=2**34, bytes_accessed=0, transcendentals=0)
SHORT = pl.CostEstimate(flops=2**29, bytes_accessed=0, transcendentals=0)
HIGHEST = lax.Precision.HIGHEST
VMEM = pl.BlockSpec(memory_space=pltpu.VMEM)
HBM = pl.BlockSpec(memory_space=pltpu.HBM)
F32 = jnp.float32
BF16 = jnp.bfloat16


def call(kernel, outputs, name, scratch=(), in_specs=None, aliases=None, mebibytes=20, cost=None):
    def run(*args):
        specs = in_specs or [VMEM] * len(args)
        return pl.pallas_call(
            kernel,
            out_shape=[jax.ShapeDtypeStruct(shape, dtype) for shape, dtype in outputs],
            in_specs=specs,
            out_specs=[VMEM] * len(outputs),
            scratch_shapes=scratch,
            compiler_params=pltpu.CompilerParams(vmem_limit_bytes=mebibytes * 2**20),
            cost_estimate=cost,
            input_output_aliases=aliases or {},
            name=name,
        )(*args)

    return run


def split(value, terms=2):
    parts = []
    for _ in range(terms):
        parts.append(value.astype(BF16))
        value = value - parts[-1].astype(F32)
    return jnp.concatenate(parts, axis=0)


def join(value, terms=2):
    height = value.shape[0] // terms
    result = value[-height:]
    for term in range(terms - 2, -1, -1):
        result = value[term * height : (term + 1) * height] + result
    return result


def total(*refs):
    terms = [ref[...].astype(F32) for ref in refs]
    while len(terms) > 1:
        terms = [sum(terms[i + 1 : i + 2], terms[i]) for i in range(0, len(terms), 2)]
    return terms[0]


def contract_last(left, right, precision=None):
    return lax.dot_general(
        left, right, (((1,), (1,)), ((), ())), preferred_element_type=F32, precision=precision
    )


def position():
    return lax.rem(lax.axis_index("tok"), PEERS)


def diagonal(n):
    return lax.broadcasted_iota(jnp.int32, (n, n), 0) == lax.broadcasted_iota(jnp.int32, (n, n), 1)


def core():
    return lax.rem(lax.axis_index("feat"), 2)


def aligned(index, size):
    return pl.ds(pl.multiple_of(index * size, size), size)


def fetch_kernel(rows_hbm, rows_ref, sem):
    place = aligned(1 - core(), rows_ref.shape[0] // 2)
    copy = pltpu.make_async_copy(rows_hbm.at[place, :], rows_ref.at[place, :], sem)
    copy.start()
    copy.wait()


def first_sent_kernel(basis_ref, rows_hbm, ready_ref, out_ref, rows_ref, sem):
    half = out_ref.shape[1]
    place = aligned(core(), half)
    copy = pltpu.make_async_copy(rows_hbm.at[place, :], rows_ref.at[place, :], sem)
    copy.start()
    rows = rows_ref[aligned(1 - core(), half), :]
    out_ref[...] = join(contract_last(split(basis_ref[...]), rows))
    copy.wait()


def first_kept_kernel(basis_ref, rows_ref, out_ref):
    rows = rows_ref[aligned(core(), out_ref.shape[1]), :]
    out_ref[...] = join(contract_last(split(basis_ref[...]), rows))


def projection_kernel(part, half, chunk_ref, mean_ref, rows_ref, *refs):
    out_ref = refs[-1]
    n, tokens = out_ref.shape
    place = {"all": 0, "kept": core(), "sent": 1 - core()}[half]
    place = aligned(place, tokens) if half != "all" else slice(None)
    chunk = chunk_ref[:n, :]
    shift = jnp.sum(chunk * mean_ref[n : n + 1, :], axis=1, keepdims=True)
    rows = rows_ref[place, aligned(position() ^ part, chunk.shape[1])]
    value = join(contract_last(split(chunk), rows)) - shift
    out_ref[...] = value if part == GATHER[0] else refs[0][:, place] + value


def gram_kernel(*refs):
    *refs, out_ref = refs
    n = out_ref.shape[0]
    chunks = {part: ref[:n, :] for part, ref in zip(GATHER, refs)}
    parts = [contract_last(chunks[part], chunks[part], HIGHEST) for part in range(PEERS)]
    out_ref[...] = jnp.zeros(out_ref.shape, F32)
    out_ref[:, :n] = (parts[0] + parts[1]) + (parts[2] + parts[3])


def inverse_factor_kernel(own_ref, got_ref, out_ref):
    n = own_ref.shape[0]
    gram = (own_ref[...] + got_ref[...])[:, :n]
    work = jnp.concatenate([gram, diagonal(n).astype(F32)], axis=1)
    index = lax.broadcasted_iota(jnp.int32, (n, 1), 0)
    scale = jnp.zeros((n, 1), F32)
    for k in range(n):
        pivot = work[k : k + 1, k : k + 1]
        factor = jnp.where(index > k, work[:, k : k + 1] / pivot, 0.0)
        scale = jnp.where(index == k, lax.rsqrt(pivot), scale)
        work = work - factor * work[k : k + 1, :]
    out_ref[...] = work[:, n:] * scale


def first_total_kernel(rows_in_all, own_ref, got_ref, out_ref):
    n = own_ref.shape[0] - EXTRA
    value = own_ref[...] + got_ref[...]
    mean = value[n : n + 1] / rows_in_all
    counts = jnp.where(diagonal(n), value[n + 1 : n + 2, :n], 0.0)
    counts = jnp.sum(counts, axis=1, keepdims=True)
    out_ref[:n, :] = value[:n] - counts * mean
    out_ref[n:, :] = jnp.broadcast_to(mean, (EXTRA, mean.shape[1]))


def weights_of(first, projected_ref):
    projected = projected_ref[...]
    centre = jnp.zeros((projected.shape[0], 1), F32)
    if first:
        centre = jnp.sum(projected, axis=1, keepdims=True) / projected.shape[1]
    weights = split(projected - centre if first else projected, TERMS)
    counts = join(jnp.sum(weights.astype(F32), axis=1, keepdims=True), TERMS)
    if first:
        counts = counts + centre * projected.shape[1]
        weights = jnp.concatenate([weights, jnp.ones((2 * EXTRA, projected.shape[1]), BF16)], axis=0)
    return weights, counts, centre


def image_term(first, weights, counts, centre, rows, mean_ref):
    n = counts.shape[0]
    term = jnp.dot(weights, rows, preferred_element_type=F32)
    value = join(term[: TERMS * n], TERMS)
    if not first:
        return value - counts * mean_ref[n : n + 1, :]
    sums = term[TERMS * n : TERMS * n + 1]
    counts = jnp.sum(jnp.where(diagonal(n), counts, 0.0), axis=0, keepdims=True)
    counts = jnp.concatenate([counts, jnp.zeros((1, sums.shape[1] - n), F32)], axis=1)
    below = jnp.zeros((EXTRA - 2, sums.shape[1]), F32)
    return jnp.concatenate([value + centre * sums, sums, counts, below], axis=0)


def half_image_kernel(first, own_ref, rows_ref, *refs):
    means, outs = ([None] * PEERS if first else refs[:PEERS]), refs[-PEERS:]
    tokens = aligned(core(), own_ref.shape[1])
    sides = weights_of(first, own_ref)
    for part, mean_ref, out_ref in zip(SCATTER, means, outs):
        rows = rows_ref[tokens, aligned(position() ^ part, out_ref.shape[1])]
        out_ref[...] = image_term(first, *sides, rows, mean_ref)


def image_kernel(first, other_ref, rows_ref, *refs):
    *refs, weights_ref, side_ref = refs
    peers = PEERS - 1
    means, halves, outs = ([None] * peers if first else refs[:peers]), refs[-2 * peers : -peers], refs[-peers:]
    tokens = aligned(1 - core(), other_ref.shape[1])
    weights, counts, centre = weights_of(first, other_ref)
    for part, mean_ref, half_ref, out_ref in zip(SCATTER[1:], means, halves, outs):
        rows = rows_ref[tokens, aligned(position() ^ part, out_ref.shape[1])]
        out_ref[...] = half_ref[...] + image_term(first, weights, counts, centre, rows, mean_ref)
    weights_ref[...] = weights
    side_ref[...] = jnp.broadcast_to(counts, side_ref.shape)
    side_ref[:, 1:2] = centre


def own_image_kernel(first, weights_ref, side_ref, rows_ref, half_ref, *refs):
    mean_ref, out_ref = (None if first else refs[0]), refs[-1]
    tokens = aligned(1 - core(), weights_ref.shape[1])
    rows = rows_ref[tokens, aligned(position(), out_ref.shape[1])]
    sides = weights_ref[...], side_ref[:, :1], side_ref[:, 1:2]
    out_ref[...] = half_ref[...] + image_term(first, *sides, rows, mean_ref)


def assemble_kernel(*refs):
    *chunks, out_ref = refs
    n, width = out_ref.shape[0], chunks[0].shape[1]
    for part, chunk in zip(GATHER, chunks):
        place = aligned(position() ^ part, width)
        out_ref[:, place] = chunk[:n, :]


def last_kernel(own_ref, got_ref, lower_ref, image_ref, scores_ref, basis_ref):
    n, lower = lower_ref.shape[0], lower_ref[...]
    basis_ref[...] = jnp.dot(lower, image_ref[...], preferred_element_type=F32, precision=HIGHEST)
    projected = total(own_ref, got_ref)
    projected = jnp.dot(lower, projected, preferred_element_type=F32, precision=HIGHEST)
    scores_ref[...] = jnp.sum(projected * projected, axis=0) / n


def normalised_total_kernel(own_ref, got_ref, lower_ref, out_ref):
    value = own_ref[...] + got_ref[...]
    out_ref[...] = jnp.dot(lower_ref[...], value, preferred_element_type=F32, precision=HIGHEST)


def ordered_add_kernel(own_ref, got_ref, before_ref, out_ref):
    out_ref[...] = total(own_ref, got_ref).astype(out_ref.dtype)


def add_kernel(*refs):
    refs[-1][...] = total(*refs[:-1]).astype(refs[-1].dtype)


def add(*terms, dtype=F32):
    return call(add_kernel, [(terms[0].shape, dtype)], "add")(*terms)[0]


def swap(value, axis, distance):
    size = lax.axis_size(axis)
    return lax.ppermute(value, axis, [(i, i ^ distance) for i in range(size)])


def distances(axis, start):
    step, size = start, lax.axis_size(axis)
    while step < size:
        yield step
        step *= 2


def share(value, axis):
    return [value] + [swap(value, axis, part) for part in GATHER[1:]]


def on_device(activations, start_basis):
    tokens, features = activations.shape
    n = start_basis.shape[0]
    width = features // PEERS
    rows_in_all = tokens * lax.axis_size("tok")
    last_feat = lax.axis_size("feat") // 2
    side = ((n, LANES), F32)
    half = ((n, tokens // 2), F32)
    whole = ((n, tokens), F32)

    fetched, sem = (activations.shape, BF16), [pltpu.SemaphoreType.DMA(())]
    rows = call(fetch_kernel, [fetched], "fetch", sem, in_specs=[HBM], mebibytes=46)(activations)[0]
    sent, rows = call(
        first_sent_kernel,
        [half, fetched],
        "sent_projection",
        sem,
        in_specs=[VMEM, HBM, VMEM],
        aliases={2: 1},
        mebibytes=46,
    )(start_basis, activations, rows)
    own = call(first_kept_kernel, [half], "kept_projection", cost=SHORT)(start_basis, rows)[0]
    for distance in distances("feat", 1):
        own = add(own, swap(sent if distance == 1 else own, "feat", distance))
    other = swap(own, "feat", 1)
    means, ranked, lower = [], [], []
    for step in range(ITERS):
        first, last = step == 0, step == ITERS - 1
        chunk = ((n + EXTRA if first else n, width), F32)
        weights = ((TERMS * n + 2 * EXTRA if first else TERMS * n, tokens // 2), BF16)
        kernel = functools.partial(half_image_kernel, first)
        kept, *halves = call(kernel, [chunk] * PEERS, "half_image", cost=SHORT)(own, rows, *ranked)
        kernel = functools.partial(image_kernel, first)
        *terms, weights, sums = call(kernel, [chunk] * (PEERS - 1) + [weights, side], "image")(
            other, rows, *ranked[1:], *halves
        )
        received = [swap(term, "tok", part) for part, term in zip(SCATTER[1:], terms)]
        kernel = functools.partial(own_image_kernel, first)
        kept = call(kernel, [chunk], "own_image", cost=SHORT)(weights, sums, rows, kept, *means[:1])
        image = add(*kept, *received)
        *steps, last_step = distances("tok", PEERS)
        for distance in steps:
            image = add(image, swap(image, "tok", distance))
        kernel = functools.partial(first_total_kernel, rows_in_all) if first else normalised_total_kernel
        image = call(kernel, [chunk], "total")(image, swap(image, "tok", last_step), *lower)[0]
        images = share(image, "tok")
        means = means or images
        ranked = [means[GATHER.index(part)] for part in SCATTER]
        gram = call(gram_kernel, [side], "gram")(*images)[0]
        grams = (gram, swap(gram, "feat", 1))
        before = []
        for part, image, mean in zip(GATHER, images, means):
            operands = [image, mean, rows, *before]
            if part != GATHER[-1]:
                kernel = functools.partial(projection_kernel, part, "all")
                before = call(kernel, [whole], "projection", cost=SHORT)(*operands)
        if last:
            gram = add(*grams)
            kernel = functools.partial(projection_kernel, part, "all")
            own = call(kernel, [whole], "projection")(*operands, gram)[0]
            for distance in distances("feat", 1):
                terms = (own, swap(own, "feat", distance))
                if distance != last_feat:
                    narrow = ((n, tokens), BF16 if distance == last_feat // 2 else F32)
                    own = call(add_kernel, [narrow], "add")(*terms)[0]
            own, other = terms
            for distance in distances("feat", 2):
                grams = (gram, swap(gram, "feat", distance))
                gram = add(*grams)
        else:
            kernel = functools.partial(projection_kernel, part, "sent")
            sent = call(kernel, [half], "sent_projection")(*operands)[0]
            kernel = functools.partial(projection_kernel, part, "kept")
            own = call(kernel, [half], "kept_projection", cost=SHORT)(*operands)[0]
            for distance in distances("feat", 1):
                got = swap(sent if distance == 1 else own, "feat", distance)
                if distance > 1:
                    gram = add(*grams)
                    grams = (gram, swap(gram, "feat", distance))
                if distance == last_feat:
                    own = call(ordered_add_kernel, [half], "add")(own, got, gram)[0]
                else:
                    own = add(own, got)
            other = swap(own, "feat", 1)
        lower = call(inverse_factor_kernel, [((n, n), F32)], "inverse_factor", cost=LONG)(*grams)
    image = call(assemble_kernel, [((n, features), F32)], "assemble")(*images)[0]
    outputs = [((tokens,), F32), ((n, features), F32)]
    return tuple(call(last_kernel, outputs, "last")(own, other, *lower, image))


def solution(mesh):
    in_specs = (P("tok", "feat"), P(None, "feat"))
    out_specs = (P("tok"), P(None, "feat"))
    return jax.shard_map(
        on_device, mesh=mesh, in_specs=in_specs, out_specs=out_specs, check_vma=False
    )
```

```python
import functools

import jax
import jax.numpy as jnp
from jax import lax
from jax.experimental import pallas as pl
from jax.experimental.pallas import tpu as pltpu
from jax.sharding import PartitionSpec as P

ITERS = 4
PEERS = 4
LANES = 128
EXTRA = 8
SCATTER = (0, 3, 1, 2)
GATHER = (0, 3, 1, 2)
TERMS = 3
LONG = pl.CostEstimate(flops=2**34, bytes_accessed=0, transcendentals=0)
SHORT = pl.CostEstimate(flops=2**29, bytes_accessed=0, transcendentals=0)
HIGHEST = lax.Precision.HIGHEST
VMEM = pl.BlockSpec(memory_space=pltpu.VMEM)
HBM = pl.BlockSpec(memory_space=pltpu.HBM)
F32 = jnp.float32
BF16 = jnp.bfloat16


def call(kernel, outputs, name, scratch=(), in_specs=None, aliases=None, mebibytes=20, cost=None):
    def run(*args):
        specs = in_specs or [VMEM] * len(args)
        return pl.pallas_call(
            kernel,
            out_shape=[jax.ShapeDtypeStruct(shape, dtype) for shape, dtype in outputs],
            in_specs=specs,
            out_specs=[VMEM] * len(outputs),
            scratch_shapes=scratch,
            compiler_params=pltpu.CompilerParams(vmem_limit_bytes=mebibytes * 2**20),
            cost_estimate=cost,
            input_output_aliases=aliases or {},
            name=name,
        )(*args)

    return run


def split(value, terms=2):
    parts = []
    for _ in range(terms):
        parts.append(value.astype(BF16))
        value = value - parts[-1].astype(F32)
    return jnp.concatenate(parts, axis=0)


def join(value, terms=2):
    height = value.shape[0] // terms
    result = value[-height:]
    for term in range(terms - 2, -1, -1):
        result = value[term * height : (term + 1) * height] + result
    return result


def total(*refs):
    terms = [ref[...].astype(F32) for ref in refs]
    while len(terms) > 1:
        terms = [sum(terms[i + 1 : i + 2], terms[i]) for i in range(0, len(terms), 2)]
    return terms[0]


def contract_last(left, right, precision=None):
    return lax.dot_general(
        left, right, (((1,), (1,)), ((), ())), preferred_element_type=F32, precision=precision
    )


def position():
    return lax.rem(lax.axis_index("tok"), PEERS)


def diagonal(n):
    return lax.broadcasted_iota(jnp.int32, (n, n), 0) == lax.broadcasted_iota(jnp.int32, (n, n), 1)


def core():
    return lax.rem(lax.axis_index("feat"), 2)


def aligned(index, size):
    return pl.ds(pl.multiple_of(index * size, size), size)


def fetch_kernel(rows_hbm, rows_ref, sem):
    place = aligned(1 - core(), rows_ref.shape[0] // 2)
    copy = pltpu.make_async_copy(rows_hbm.at[place, :], rows_ref.at[place, :], sem)
    copy.start()
    copy.wait()


def first_sent_kernel(basis_ref, rows_hbm, ready_ref, out_ref, rows_ref, sem):
    half = out_ref.shape[1]
    place = aligned(core(), half)
    copy = pltpu.make_async_copy(rows_hbm.at[place, :], rows_ref.at[place, :], sem)
    copy.start()
    rows = rows_ref[aligned(1 - core(), half), :]
    out_ref[...] = join(contract_last(split(basis_ref[...]), rows))
    copy.wait()


def first_kept_kernel(basis_ref, rows_ref, out_ref):
    rows = rows_ref[aligned(core(), out_ref.shape[1]), :]
    out_ref[...] = join(contract_last(split(basis_ref[...]), rows))


def projection_kernel(part, half, chunk_ref, mean_ref, rows_ref, *refs):
    out_ref = refs[-1]
    n, tokens = out_ref.shape
    place = {"all": 0, "kept": core(), "sent": 1 - core()}[half]
    place = aligned(place, tokens) if half != "all" else slice(None)
    chunk = chunk_ref[:n, :]
    shift = jnp.sum(chunk * mean_ref[n : n + 1, :], axis=1, keepdims=True)
    rows = rows_ref[place, aligned(position() ^ part, chunk.shape[1])]
    value = join(contract_last(split(chunk), rows)) - shift
    out_ref[...] = value if part == GATHER[0] else refs[0][:, place] + value


def gram_kernel(*refs):
    *refs, out_ref = refs
    n = out_ref.shape[0]
    chunks = {part: ref[:n, :] for part, ref in zip(GATHER, refs)}
    parts = [contract_last(chunks[part], chunks[part], HIGHEST) for part in range(PEERS)]
    out_ref[...] = jnp.zeros(out_ref.shape, F32)
    out_ref[:, :n] = (parts[0] + parts[1]) + (parts[2] + parts[3])


def inverse_factor_kernel(own_ref, got_ref, out_ref):
    n = own_ref.shape[0]
    gram = (own_ref[...] + got_ref[...])[:, :n]
    work = jnp.concatenate([gram, diagonal(n).astype(F32)], axis=1)
    index = lax.broadcasted_iota(jnp.int32, (n, 1), 0)
    scale = jnp.zeros((n, 1), F32)
    for k in range(n):
        pivot = work[k : k + 1, k : k + 1]
        factor = jnp.where(index > k, work[:, k : k + 1] / pivot, 0.0)
        scale = jnp.where(index == k, lax.rsqrt(pivot), scale)
        work = work - factor * work[k : k + 1, :]
    out_ref[...] = work[:, n:] * scale


def first_total_kernel(rows_in_all, own_ref, got_ref, out_ref):
    n = own_ref.shape[0] - EXTRA
    value = own_ref[...] + got_ref[...]
    mean = value[n : n + 1] / rows_in_all
    counts = jnp.where(diagonal(n), value[n + 1 : n + 2, :n], 0.0)
    counts = jnp.sum(counts, axis=1, keepdims=True)
    out_ref[:n, :] = value[:n] - counts * mean
    out_ref[n:, :] = jnp.broadcast_to(mean, (EXTRA, mean.shape[1]))


def weights_of(first, projected_ref):
    projected = projected_ref[...]
    centre = jnp.zeros((projected.shape[0], 1), F32)
    if first:
        centre = jnp.sum(projected, axis=1, keepdims=True) / projected.shape[1]
    weights = split(projected - centre if first else projected, TERMS)
    counts = join(jnp.sum(weights.astype(F32), axis=1, keepdims=True), TERMS)
    if first:
        counts = counts + centre * projected.shape[1]
        weights = jnp.concatenate([weights, jnp.ones((2 * EXTRA, projected.shape[1]), BF16)], axis=0)
    return weights, counts, centre


def image_term(first, weights, counts, centre, rows, mean_ref):
    n = counts.shape[0]
    term = jnp.dot(weights, rows, preferred_element_type=F32)
    value = join(term[: TERMS * n], TERMS)
    if not first:
        return value - counts * mean_ref[n : n + 1, :]
    sums = term[TERMS * n : TERMS * n + 1]
    counts = jnp.sum(jnp.where(diagonal(n), counts, 0.0), axis=0, keepdims=True)
    counts = jnp.concatenate([counts, jnp.zeros((1, sums.shape[1] - n), F32)], axis=1)
    below = jnp.zeros((EXTRA - 2, sums.shape[1]), F32)
    return jnp.concatenate([value + centre * sums, sums, counts, below], axis=0)


def half_image_kernel(first, own_ref, rows_ref, *refs):
    means, outs = ([None] * PEERS if first else refs[:PEERS]), refs[-PEERS:]
    tokens = aligned(core(), own_ref.shape[1])
    sides = weights_of(first, own_ref)
    for part, mean_ref, out_ref in zip(SCATTER, means, outs):
        rows = rows_ref[tokens, aligned(position() ^ part, out_ref.shape[1])]
        out_ref[...] = image_term(first, *sides, rows, mean_ref)


def image_kernel(first, other_ref, rows_ref, *refs):
    *refs, weights_ref, side_ref = refs
    peers = PEERS - 1
    means, halves, outs = ([None] * peers if first else refs[:peers]), refs[-2 * peers : -peers], refs[-peers:]
    tokens = aligned(1 - core(), other_ref.shape[1])
    weights, counts, centre = weights_of(first, other_ref)
    for part, mean_ref, half_ref, out_ref in zip(SCATTER[1:], means, halves, outs):
        rows = rows_ref[tokens, aligned(position() ^ part, out_ref.shape[1])]
        out_ref[...] = half_ref[...] + image_term(first, weights, counts, centre, rows, mean_ref)
    weights_ref[...] = weights
    side_ref[...] = jnp.broadcast_to(counts, side_ref.shape)
    side_ref[:, 1:2] = centre


def own_image_kernel(first, weights_ref, side_ref, rows_ref, half_ref, *refs):
    mean_ref, out_ref = (None if first else refs[0]), refs[-1]
    tokens = aligned(1 - core(), weights_ref.shape[1])
    rows = rows_ref[tokens, aligned(position(), out_ref.shape[1])]
    sides = weights_ref[...], side_ref[:, :1], side_ref[:, 1:2]
    out_ref[...] = half_ref[...] + image_term(first, *sides, rows, mean_ref)


def assemble_kernel(*refs):
    *chunks, out_ref = refs
    n, width = out_ref.shape[0], chunks[0].shape[1]
    for part, chunk in zip(GATHER, chunks):
        place = aligned(position() ^ part, width)
        out_ref[:, place] = chunk[:n, :]


def last_kernel(own_ref, got_ref, lower_ref, image_ref, scores_ref, basis_ref):
    n, lower = lower_ref.shape[0], lower_ref[...]
    basis_ref[...] = jnp.dot(lower, image_ref[...], preferred_element_type=F32, precision=HIGHEST)
    projected = total(own_ref, got_ref)
    projected = jnp.dot(lower, projected, preferred_element_type=F32, precision=HIGHEST)
    scores_ref[...] = jnp.sum(projected * projected, axis=0) / n


def normalised_total_kernel(own_ref, got_ref, lower_ref, out_ref):
    value = own_ref[...] + got_ref[...]
    out_ref[...] = jnp.dot(lower_ref[...], value, preferred_element_type=F32, precision=HIGHEST)


def ordered_copy_kernel(value_ref, before_ref, out_ref):
    out_ref[...] = value_ref[...]


def ordered_add_kernel(own_ref, got_ref, before_ref, out_ref):
    out_ref[...] = total(own_ref, got_ref).astype(out_ref.dtype)


def add_kernel(*refs):
    refs[-1][...] = total(*refs[:-1]).astype(refs[-1].dtype)


def add(*terms, dtype=F32):
    return call(add_kernel, [(terms[0].shape, dtype)], "add")(*terms)[0]


def swap(value, axis, distance):
    size = lax.axis_size(axis)
    return lax.ppermute(value, axis, [(i, i ^ distance) for i in range(size)])


def distances(axis, start):
    step, size = start, lax.axis_size(axis)
    while step < size:
        yield step
        step *= 2


def share(value, axis):
    return [value] + [swap(value, axis, part) for part in GATHER[1:]]


def on_device(activations, start_basis):
    tokens, features = activations.shape
    n = start_basis.shape[0]
    width = features // PEERS
    rows_in_all = tokens * lax.axis_size("tok")
    last_feat = lax.axis_size("feat") // 2
    side = ((n, LANES), F32)
    half = ((n, tokens // 2), F32)
    whole = ((n, tokens), F32)

    fetched, sem = (activations.shape, BF16), [pltpu.SemaphoreType.DMA(())]
    rows = call(fetch_kernel, [fetched], "fetch", sem, in_specs=[HBM], mebibytes=46)(activations)[0]
    sent, rows = call(
        first_sent_kernel,
        [half, fetched],
        "sent_projection",
        sem,
        in_specs=[VMEM, HBM, VMEM],
        aliases={2: 1},
        mebibytes=46,
    )(start_basis, activations, rows)
    own = call(first_kept_kernel, [half], "kept_projection", cost=SHORT)(start_basis, rows)[0]
    for distance in distances("feat", 1):
        own = add(own, swap(sent if distance == 1 else own, "feat", distance))
    other = swap(own, "feat", 1)
    means, ranked, lower = [], [], []
    for step in range(ITERS):
        first, last = step == 0, step == ITERS - 1
        chunk = ((n + EXTRA if first else n, width), F32)
        weights = ((TERMS * n + 2 * EXTRA if first else TERMS * n, tokens // 2), BF16)
        kernel = functools.partial(half_image_kernel, first)
        kept, *halves = call(kernel, [chunk] * PEERS, "half_image", cost=SHORT)(own, rows, *ranked)
        kernel = functools.partial(image_kernel, first)
        *terms, weights, sums = call(kernel, [chunk] * (PEERS - 1) + [weights, side], "image")(
            other, rows, *ranked[1:], *halves
        )
        received = [swap(term, "tok", part) for part, term in zip(SCATTER[1:], terms)]
        kernel = functools.partial(own_image_kernel, first)
        kept = call(kernel, [chunk], "own_image", cost=SHORT)(weights, sums, rows, kept, *means[:1])
        image = add(*kept, *received)
        *steps, last_step = distances("tok", PEERS)
        for distance in steps:
            image = add(image, swap(image, "tok", distance))
        kernel = functools.partial(first_total_kernel, rows_in_all) if first else normalised_total_kernel
        image = call(kernel, [chunk], "total")(image, swap(image, "tok", last_step), *lower)[0]
        images = share(image, "tok")
        means = means or images
        ranked = [means[GATHER.index(part)] for part in SCATTER]
        before = []
        for part, image, mean in zip(GATHER, images, means):
            operands = [image, mean, rows, *before]
            if part != GATHER[-1]:
                kernel = functools.partial(projection_kernel, part, "all")
                before = call(kernel, [whole], "projection", cost=SHORT)(*operands)
            if part == GATHER[1]:
                ready = before if last else []
        gram = call(gram_kernel, [side], "gram")(*images, *ready)[0]
        grams = (gram, swap(gram, "feat", 1))
        if last:
            gram = add(*grams)
            kernel = functools.partial(projection_kernel, part, "all")
            own = call(kernel, [whole], "projection", cost=SHORT)(*operands)[0]
            own = call(ordered_copy_kernel, [whole], "copy")(own, gram)[0]
            for distance in distances("feat", 1):
                terms = (own, swap(own, "feat", distance))
                if distance != last_feat:
                    narrow = ((n, tokens), BF16 if distance == last_feat // 2 else F32)
                    own = call(add_kernel, [narrow], "add")(*terms)[0]
            own, other = terms
            for distance in distances("feat", 2):
                grams = (gram, swap(gram, "feat", distance))
                gram = add(*grams)
        else:
            kernel = functools.partial(projection_kernel, part, "sent")
            sent = call(kernel, [half], "sent_projection")(*operands)[0]
            kernel = functools.partial(projection_kernel, part, "kept")
            own = call(kernel, [half], "kept_projection", cost=SHORT)(*operands)[0]
            for distance in distances("feat", 1):
                got = swap(sent if distance == 1 else own, "feat", distance)
                if distance > 1:
                    gram = add(*grams)
                    grams = (gram, swap(gram, "feat", distance))
                if distance == last_feat:
                    own = call(ordered_add_kernel, [half], "add")(own, got, gram)[0]
                else:
                    own = add(own, got)
            other = swap(own, "feat", 1)
        lower = call(inverse_factor_kernel, [((n, n), F32)], "inverse_factor", cost=LONG)(*grams)
    image = call(assemble_kernel, [((n, features), F32)], "assemble")(*images)[0]
    outputs = [((tokens,), F32), ((n, features), F32)]
    return tuple(call(last_kernel, outputs, "last")(own, other, *lower, image))


def solution(mesh):
    in_specs = (P("tok", "feat"), P(None, "feat"))
    out_specs = (P("tok"), P(None, "feat"))
    return jax.shard_map(
        on_device, mesh=mesh, in_specs=in_specs, out_specs=out_specs, check_vma=False
    )
```

```python
import functools

import jax
import jax.numpy as jnp
from jax import lax
from jax.experimental import pallas as pl
from jax.experimental.pallas import tpu as pltpu
from jax.sharding import PartitionSpec as P

ITERS = 4
PEERS = 4
LANES = 128
EXTRA = 8
SCATTER = (0, 3, 1, 2)
GATHER = (0, 3, 1, 2)
TERMS = 3
LONG = pl.CostEstimate(flops=2**34, bytes_accessed=0, transcendentals=0)
SHORT = pl.CostEstimate(flops=2**29, bytes_accessed=0, transcendentals=0)
HIGHEST = lax.Precision.HIGHEST
VMEM = pl.BlockSpec(memory_space=pltpu.VMEM)
HBM = pl.BlockSpec(memory_space=pltpu.HBM)
F32 = jnp.float32
BF16 = jnp.bfloat16


def call(kernel, outputs, name, scratch=(), in_specs=None, aliases=None, mebibytes=20, cost=None):
    def run(*args):
        specs = in_specs or [VMEM] * len(args)
        return pl.pallas_call(
            kernel,
            out_shape=[jax.ShapeDtypeStruct(shape, dtype) for shape, dtype in outputs],
            in_specs=specs,
            out_specs=[VMEM] * len(outputs),
            scratch_shapes=scratch,
            compiler_params=pltpu.CompilerParams(vmem_limit_bytes=mebibytes * 2**20),
            cost_estimate=cost,
            input_output_aliases=aliases or {},
            name=name,
        )(*args)

    return run


def split(value, terms=2):
    parts = []
    for _ in range(terms):
        parts.append(value.astype(BF16))
        value = value - parts[-1].astype(F32)
    return jnp.concatenate(parts, axis=0)


def join(value, terms=2):
    height = value.shape[0] // terms
    result = value[-height:]
    for term in range(terms - 2, -1, -1):
        result = value[term * height : (term + 1) * height] + result
    return result


def total(*refs):
    terms = [ref[...].astype(F32) for ref in refs]
    while len(terms) > 1:
        terms = [sum(terms[i + 1 : i + 2], terms[i]) for i in range(0, len(terms), 2)]
    return terms[0]


def terms_of(value):
    parts = []
    for _ in range(3):
        parts.append(value.astype(BF16))
        value = value - parts[-1].astype(F32)
    return parts


def stacked(value):
    high, middle, low = terms_of(value)
    return jnp.concatenate([high, middle, low, high, middle, high], axis=0)


def product(left, right_stacked):
    high, middle, low = terms_of(left)
    left = jnp.concatenate([high, high, high, middle, middle, low], axis=1)
    return jnp.dot(left, right_stacked, preferred_element_type=F32)


def contract_last(left, right, precision=None):
    return lax.dot_general(
        left, right, (((1,), (1,)), ((), ())), preferred_element_type=F32, precision=precision
    )


def position():
    return lax.rem(lax.axis_index("tok"), PEERS)


def diagonal(n):
    return lax.broadcasted_iota(jnp.int32, (n, n), 0) == lax.broadcasted_iota(jnp.int32, (n, n), 1)


def core():
    index, parity, shift = lax.axis_index("feat"), 0, 1
    while shift < lax.axis_size("feat"):
        parity = parity + lax.rem(index // shift, 2)
        shift *= 2
    return lax.rem(parity, 2)


def aligned(index, size):
    return pl.ds(pl.multiple_of(index * size, size), size)


def fetch_kernel(rows_hbm, rows_ref, sem):
    place = aligned(1 - core(), rows_ref.shape[0] // 2)
    copy = pltpu.make_async_copy(rows_hbm.at[place, :], rows_ref.at[place, :], sem)
    copy.start()
    copy.wait()


def first_sent_kernel(basis_ref, rows_hbm, ready_ref, out_ref, rows_ref, sem):
    half = out_ref.shape[1]
    place = aligned(core(), half)
    copy = pltpu.make_async_copy(rows_hbm.at[place, :], rows_ref.at[place, :], sem)
    copy.start()
    rows = rows_ref[aligned(1 - core(), half), :]
    out_ref[...] = join(contract_last(split(basis_ref[...]), rows))
    copy.wait()


def first_kept_kernel(basis_ref, rows_ref, out_ref):
    rows = rows_ref[aligned(core(), out_ref.shape[1]), :]
    out_ref[...] = join(contract_last(split(basis_ref[...]), rows))


def projection_kernel(part, half, chunk_ref, mean_ref, rows_ref, *refs):
    out_ref = refs[-1]
    n, tokens = out_ref.shape
    place = {"all": 0, "kept": core(), "sent": 1 - core()}[half]
    place = aligned(place, tokens) if half != "all" else slice(None)
    chunk = chunk_ref[:n, :]
    shift = jnp.sum(chunk * mean_ref[n : n + 1, :], axis=1, keepdims=True)
    rows = rows_ref[place, aligned(position() ^ part, chunk.shape[1])]
    value = join(contract_last(split(chunk), rows)) - shift
    out_ref[...] = value if part == GATHER[0] else refs[0][:, place] + value


def gram_kernel(*refs):
    *refs, out_ref = refs
    n = out_ref.shape[0]
    chunks = {part: ref[:n, :] for part, ref in zip(GATHER, refs)}
    parts = [contract_last(chunks[part], chunks[part], HIGHEST) for part in range(PEERS)]
    out_ref[...] = jnp.zeros(out_ref.shape, F32)
    out_ref[:, :n] = (parts[0] + parts[1]) + (parts[2] + parts[3])


def inverse_factor_kernel(own_ref, got_ref, out_ref):
    n = own_ref.shape[0]
    gram = (own_ref[...] + got_ref[...])[:, :n]
    work = jnp.concatenate([gram, diagonal(n).astype(F32)], axis=1)
    index = lax.broadcasted_iota(jnp.int32, (n, 1), 0)
    scale = jnp.zeros((n, 1), F32)
    for k in range(n):
        pivot = work[k : k + 1, k : k + 1]
        factor = jnp.where(index > k, work[:, k : k + 1] / pivot, 0.0)
        scale = jnp.where(index == k, lax.rsqrt(pivot), scale)
        work = work - factor * work[k : k + 1, :]
    out_ref[...] = work[:, n:] * scale


def first_total_kernel(rows_in_all, own_ref, got_ref, out_ref):
    n = own_ref.shape[0] - EXTRA
    value = own_ref[...] + got_ref[...]
    mean = value[n : n + 1] / rows_in_all
    counts = jnp.where(diagonal(n), value[n + 1 : n + 2, :n], 0.0)
    counts = jnp.sum(counts, axis=1, keepdims=True)
    out_ref[:n, :] = value[:n] - counts * mean
    out_ref[n:, :] = jnp.broadcast_to(mean, (EXTRA, mean.shape[1]))


def weights_of(first, projected_ref):
    projected = projected_ref[...]
    centre = jnp.zeros((projected.shape[0], 1), F32)
    if first:
        centre = jnp.sum(projected, axis=1, keepdims=True) / projected.shape[1]
    weights = split(projected - centre if first else projected, TERMS)
    counts = join(jnp.sum(weights.astype(F32), axis=1, keepdims=True), TERMS)
    if first:
        counts = counts + centre * projected.shape[1]
        weights = jnp.concatenate([weights, jnp.ones((2 * EXTRA, projected.shape[1]), BF16)], axis=0)
    return weights, counts, centre


def image_term(first, weights, counts, centre, rows, mean_ref):
    n = counts.shape[0]
    term = jnp.dot(weights, rows, preferred_element_type=F32)
    value = join(term[: TERMS * n], TERMS)
    if not first:
        return value - counts * mean_ref[n : n + 1, :]
    sums = term[TERMS * n : TERMS * n + 1]
    counts = jnp.sum(jnp.where(diagonal(n), counts, 0.0), axis=0, keepdims=True)
    counts = jnp.concatenate([counts, jnp.zeros((1, sums.shape[1] - n), F32)], axis=1)
    below = jnp.zeros((EXTRA - 2, sums.shape[1]), F32)
    return jnp.concatenate([value + centre * sums, sums, counts, below], axis=0)


def half_image_kernel(first, own_ref, rows_ref, *refs):
    means, outs = ([None] * PEERS if first else refs[:PEERS]), refs[-PEERS:]
    tokens = aligned(core(), own_ref.shape[1])
    sides = weights_of(first, own_ref)
    for part, mean_ref, out_ref in zip(SCATTER, means, outs):
        rows = rows_ref[tokens, aligned(position() ^ part, out_ref.shape[1])]
        out_ref[...] = image_term(first, *sides, rows, mean_ref)


def image_kernel(first, other_ref, rows_ref, *refs):
    *refs, weights_ref, side_ref = refs
    peers = PEERS - 1
    means, halves, outs = ([None] * peers if first else refs[:peers]), refs[-2 * peers : -peers], refs[-peers:]
    tokens = aligned(1 - core(), other_ref.shape[1])
    weights, counts, centre = weights_of(first, other_ref)
    for part, mean_ref, half_ref, out_ref in zip(SCATTER[1:], means, halves, outs):
        rows = rows_ref[tokens, aligned(position() ^ part, out_ref.shape[1])]
        out_ref[...] = half_ref[...] + image_term(first, weights, counts, centre, rows, mean_ref)
    weights_ref[...] = weights
    side_ref[...] = jnp.broadcast_to(counts, side_ref.shape)
    side_ref[:, 1:2] = centre


def own_image_kernel(first, weights_ref, side_ref, rows_ref, half_ref, *refs):
    mean_ref, out_ref = (None if first else refs[0]), refs[-1]
    tokens = aligned(1 - core(), weights_ref.shape[1])
    rows = rows_ref[tokens, aligned(position(), out_ref.shape[1])]
    sides = weights_ref[...], side_ref[:, :1], side_ref[:, 1:2]
    out_ref[...] = half_ref[...] + image_term(first, *sides, rows, mean_ref)


def assemble_kernel(*refs):
    *chunks, out_ref = refs
    width = chunks[0].shape[1]
    for part, chunk in zip(GATHER, chunks):
        out_ref[:, aligned(position() ^ part, width)] = stacked(chunk[...])


def last_kernel(own_ref, got_ref, lower_ref, image_ref, scores_ref, basis_ref):
    n, lower = lower_ref.shape[0], lower_ref[...]
    basis_ref[...] = product(lower, image_ref[...])
    projected = product(lower, stacked(total(own_ref, got_ref)))
    scores_ref[...] = jnp.sum(projected * projected, axis=0) / n


def normalised_total_kernel(own_ref, got_ref, lower_ref, out_ref):
    value = own_ref[...] + got_ref[...]
    out_ref[...] = product(lower_ref[...], stacked(value))


def ordered_copy_kernel(value_ref, before_ref, out_ref):
    out_ref[...] = value_ref[...]


def ordered_add_kernel(own_ref, got_ref, before_ref, out_ref):
    out_ref[...] = total(own_ref, got_ref).astype(out_ref.dtype)


def add_kernel(*refs):
    refs[-1][...] = total(*refs[:-1]).astype(refs[-1].dtype)


def add(*terms, dtype=F32):
    return call(add_kernel, [(terms[0].shape, dtype)], "add")(*terms)[0]


def swap(value, axis, distance):
    size = lax.axis_size(axis)
    if axis == "feat" and distance > 1:
        distance += 1
    return lax.ppermute(value, axis, [(i, i ^ distance) for i in range(size)])


def distances(axis, start):
    step, size = start, lax.axis_size(axis)
    while step < size:
        yield step
        step *= 2


def share(value, axis):
    return [value] + [swap(value, axis, part) for part in GATHER[1:]]


def on_device(activations, start_basis):
    tokens, features = activations.shape
    n = start_basis.shape[0]
    width = features // PEERS
    rows_in_all = tokens * lax.axis_size("tok")
    last_feat = lax.axis_size("feat") // 2
    side = ((n, LANES), F32)
    half = ((n, tokens // 2), F32)
    whole = ((n, tokens), F32)

    fetched, sem = (activations.shape, BF16), [pltpu.SemaphoreType.DMA(())]
    rows = call(fetch_kernel, [fetched], "fetch", sem, in_specs=[HBM], mebibytes=46)(activations)[0]
    sent, rows = call(
        first_sent_kernel,
        [half, fetched],
        "sent_projection",
        sem,
        in_specs=[VMEM, HBM, VMEM],
        aliases={2: 1},
        mebibytes=46,
    )(start_basis, activations, rows)
    own = call(first_kept_kernel, [half], "kept_projection", cost=SHORT)(start_basis, rows)[0]
    for distance in distances("feat", 1):
        own = add(own, swap(sent if distance == 1 else own, "feat", distance))
    other = swap(own, "feat", 1)
    means, ranked, lower = [], [], []
    for step in range(ITERS):
        first, last = step == 0, step == ITERS - 1
        chunk = ((n + EXTRA if first else n, width), F32)
        weights = ((TERMS * n + 2 * EXTRA if first else TERMS * n, tokens // 2), BF16)
        kernel = functools.partial(half_image_kernel, first)
        kept, *halves = call(kernel, [chunk] * PEERS, "half_image", cost=SHORT)(own, rows, *ranked)
        kernel = functools.partial(image_kernel, first)
        *terms, weights, sums = call(kernel, [chunk] * (PEERS - 1) + [weights, side], "image")(
            other, rows, *ranked[1:], *halves
        )
        received = [swap(term, "tok", part) for part, term in zip(SCATTER[1:], terms)]
        kernel = functools.partial(own_image_kernel, first)
        kept = call(kernel, [chunk], "own_image", cost=SHORT)(weights, sums, rows, kept, *means[:1])
        image = add(*kept, *received)
        *steps, last_step = distances("tok", PEERS)
        for distance in steps:
            image = add(image, swap(image, "tok", distance))
        kernel = functools.partial(first_total_kernel, rows_in_all) if first else normalised_total_kernel
        image = call(kernel, [chunk], "total")(image, swap(image, "tok", last_step), *lower)[0]
        images = share(image, "tok")
        means = means or images
        ranked = [means[GATHER.index(part)] for part in SCATTER]
        before = []
        for part, image, mean in zip(GATHER, images, means):
            operands = [image, mean, rows, *before]
            if part != GATHER[-1]:
                kernel = functools.partial(projection_kernel, part, "all")
                before = call(kernel, [whole], "projection", cost=SHORT)(*operands)
            if part == GATHER[1]:
                ready = before if last else []
        gram = call(gram_kernel, [side], "gram")(*images, *ready)[0]
        grams = (gram, swap(gram, "feat", 1))
        if last:
            gram = add(*grams)
            kernel = functools.partial(projection_kernel, part, "all")
            own = call(kernel, [whole], "projection", cost=SHORT)(*operands)[0]
            own = call(ordered_copy_kernel, [whole], "copy")(own, gram)[0]
            for distance in distances("feat", 1):
                terms = (own, swap(own, "feat", distance))
                if distance != last_feat:
                    narrow = ((n, tokens), BF16 if distance == last_feat // 2 else F32)
                    own = call(add_kernel, [narrow], "add")(*terms)[0]
            own, other = terms
            for distance in distances("feat", 2):
                grams = (gram, swap(gram, "feat", distance))
                gram = add(*grams)
        else:
            kernel = functools.partial(projection_kernel, part, "sent")
            sent = call(kernel, [half], "sent_projection")(*operands)[0]
            kernel = functools.partial(projection_kernel, part, "kept")
            own = call(kernel, [half], "kept_projection", cost=SHORT)(*operands)[0]
            for distance in distances("feat", 1):
                got = swap(sent if distance == 1 else own, "feat", distance)
                if distance > 1:
                    gram = add(*grams)
                    grams = (gram, swap(gram, "feat", distance))
                if distance == last_feat:
                    own = call(ordered_add_kernel, [half], "add")(own, got, gram)[0]
                else:
                    own = add(own, got)
            other = swap(own, "feat", 1)
        lower = call(inverse_factor_kernel, [((n, n), F32)], "inverse_factor", cost=LONG)(*grams)
    image = call(assemble_kernel, [((6 * n, features), BF16)], "assemble")(*images)[0]
    outputs = [((tokens,), F32), ((n, features), F32)]
    return tuple(call(last_kernel, outputs, "last")(own, other, *lower, image))


def solution(mesh):
    in_specs = (P("tok", "feat"), P(None, "feat"))
    out_specs = (P("tok"), P(None, "feat"))
    return jax.shard_map(
        on_device, mesh=mesh, in_specs=in_specs, out_specs=out_specs, check_vma=False
    )
```

```python
import functools

import jax
import jax.numpy as jnp
from jax import lax
from jax.experimental import pallas as pl
from jax.experimental.pallas import tpu as pltpu
from jax.sharding import PartitionSpec as P

ITERS = 4
PEERS = 4
LANES = 128
EXTRA = 8
SCATTER = (0, 3, 1, 2)
GATHER = (0, 3, 1, 2)
TERMS = 3
LONG = pl.CostEstimate(flops=2**34, bytes_accessed=0, transcendentals=0)
SHORT = pl.CostEstimate(flops=2**29, bytes_accessed=0, transcendentals=0)
HIGHEST = lax.Precision.HIGHEST
VMEM = pl.BlockSpec(memory_space=pltpu.VMEM)
HBM = pl.BlockSpec(memory_space=pltpu.HBM)
F32 = jnp.float32
BF16 = jnp.bfloat16


def call(kernel, outputs, name, scratch=(), in_specs=None, aliases=None, mebibytes=20, cost=None):
    def run(*args):
        specs = in_specs or [VMEM] * len(args)
        return pl.pallas_call(
            kernel,
            out_shape=[jax.ShapeDtypeStruct(shape, dtype) for shape, dtype in outputs],
            in_specs=specs,
            out_specs=[VMEM] * len(outputs),
            scratch_shapes=scratch,
            compiler_params=pltpu.CompilerParams(vmem_limit_bytes=mebibytes * 2**20),
            cost_estimate=cost,
            input_output_aliases=aliases or {},
            name=name,
        )(*args)

    return run


def split(value, terms=2):
    parts = []
    for _ in range(terms):
        parts.append(value.astype(BF16))
        value = value - parts[-1].astype(F32)
    return jnp.concatenate(parts, axis=0)


def join(value, terms=2):
    height = value.shape[0] // terms
    result = value[-height:]
    for term in range(terms - 2, -1, -1):
        result = value[term * height : (term + 1) * height] + result
    return result


def total(*refs):
    terms = [ref[...].astype(F32) for ref in refs]
    while len(terms) > 1:
        terms = [sum(terms[i + 1 : i + 2], terms[i]) for i in range(0, len(terms), 2)]
    return terms[0]


def terms_of(value):
    parts = []
    for _ in range(3):
        parts.append(value.astype(BF16))
        value = value - parts[-1].astype(F32)
    return parts


def stacked(value):
    high, middle, low = terms_of(value)
    return jnp.concatenate([high, middle, low, high, middle, high], axis=0)


def product(left, right_stacked):
    high, middle, low = terms_of(left)
    left = jnp.concatenate([high, high, high, middle, middle, low], axis=1)
    return jnp.dot(left, right_stacked, preferred_element_type=F32)


def contract_last(left, right, precision=None):
    return lax.dot_general(
        left, right, (((1,), (1,)), ((), ())), preferred_element_type=F32, precision=precision
    )


def position():
    return lax.rem(lax.axis_index("tok"), PEERS)


def diagonal(n):
    return lax.broadcasted_iota(jnp.int32, (n, n), 0) == lax.broadcasted_iota(jnp.int32, (n, n), 1)


def core():
    index, parity, shift = lax.axis_index("feat"), 0, 1
    while shift < lax.axis_size("feat"):
        parity = parity + lax.rem(index // shift, 2)
        shift *= 2
    return lax.rem(parity, 2)


def aligned(index, size):
    return pl.ds(pl.multiple_of(index * size, size), size)


def fetch_kernel(rows_hbm, rows_ref, sem):
    place = aligned(1 - core(), rows_ref.shape[0] // 2)
    copy = pltpu.make_async_copy(rows_hbm.at[place, :], rows_ref.at[place, :], sem)
    copy.start()
    copy.wait()


def first_sent_kernel(basis_ref, rows_hbm, ready_ref, out_ref, rows_ref, sem):
    half = out_ref.shape[1]
    place = aligned(core(), half)
    copy = pltpu.make_async_copy(rows_hbm.at[place, :], rows_ref.at[place, :], sem)
    copy.start()
    rows = rows_ref[aligned(1 - core(), half), :]
    out_ref[...] = join(contract_last(split(basis_ref[...]), rows))
    copy.wait()


def first_kept_kernel(basis_ref, rows_ref, out_ref):
    rows = rows_ref[aligned(core(), out_ref.shape[1]), :]
    out_ref[...] = join(contract_last(split(basis_ref[...]), rows))


def projection_kernel(part, half, chunk_ref, mean_ref, rows_ref, *refs):
    out_ref = refs[-1]
    n, tokens = out_ref.shape
    place = {"all": 0, "kept": core(), "sent": 1 - core()}[half]
    place = aligned(place, tokens) if half != "all" else slice(None)
    chunk = chunk_ref[:n, :].astype(F32)
    shift = jnp.sum(chunk * mean_ref[n : n + 1, :], axis=1, keepdims=True)
    rows = rows_ref[place, aligned(position() ^ part, chunk.shape[1])]
    value = join(contract_last(split(chunk), rows)) - shift
    out_ref[...] = value if part == GATHER[0] else refs[0][:, place] + value


def gram_kernel(*refs):
    *refs, out_ref = refs
    n = out_ref.shape[0]
    chunks = {part: ref[:n, :].astype(F32) for part, ref in zip(GATHER, refs)}
    parts = [contract_last(chunks[part], chunks[part], HIGHEST) for part in range(PEERS)]
    out_ref[...] = jnp.zeros(out_ref.shape, F32)
    out_ref[:, :n] = (parts[0] + parts[1]) + (parts[2] + parts[3])


def inverse_factor_kernel(own_ref, got_ref, out_ref):
    n = own_ref.shape[0]
    gram = (own_ref[...] + got_ref[...])[:, :n]
    work = jnp.concatenate([gram, diagonal(n).astype(F32)], axis=1)
    index = lax.broadcasted_iota(jnp.int32, (n, 1), 0)
    scale = jnp.zeros((n, 1), F32)
    for k in range(n):
        pivot = work[k : k + 1, k : k + 1]
        factor = jnp.where(index > k, work[:, k : k + 1] / pivot, 0.0)
        scale = jnp.where(index == k, lax.rsqrt(pivot), scale)
        work = work - factor * work[k : k + 1, :]
    out_ref[...] = work[:, n:] * scale


def first_total_kernel(rows_in_all, own_ref, got_ref, out_ref):
    n = own_ref.shape[0] - EXTRA
    value = own_ref[...] + got_ref[...]
    mean = value[n : n + 1] / rows_in_all
    counts = jnp.where(diagonal(n), value[n + 1 : n + 2, :n], 0.0)
    counts = jnp.sum(counts, axis=1, keepdims=True)
    out_ref[:n, :] = value[:n] - counts * mean
    out_ref[n:, :] = jnp.broadcast_to(mean, (EXTRA, mean.shape[1]))


def weights_of(first, projected_ref):
    projected = projected_ref[...]
    centre = jnp.zeros((projected.shape[0], 1), F32)
    if first:
        centre = jnp.sum(projected, axis=1, keepdims=True) / projected.shape[1]
    weights = split(projected - centre if first else projected, TERMS)
    counts = join(jnp.sum(weights.astype(F32), axis=1, keepdims=True), TERMS)
    if first:
        counts = counts + centre * projected.shape[1]
        weights = jnp.concatenate([weights, jnp.ones((2 * EXTRA, projected.shape[1]), BF16)], axis=0)
    return weights, counts, centre


def image_term(first, weights, counts, centre, rows, mean_ref):
    n = counts.shape[0]
    term = jnp.dot(weights, rows, preferred_element_type=F32)
    value = join(term[: TERMS * n], TERMS)
    if not first:
        return value - counts * mean_ref[n : n + 1, :]
    sums = term[TERMS * n : TERMS * n + 1]
    counts = jnp.sum(jnp.where(diagonal(n), counts, 0.0), axis=0, keepdims=True)
    counts = jnp.concatenate([counts, jnp.zeros((1, sums.shape[1] - n), F32)], axis=1)
    below = jnp.zeros((EXTRA - 2, sums.shape[1]), F32)
    return jnp.concatenate([value + centre * sums, sums, counts, below], axis=0)


def half_image_kernel(first, own_ref, rows_ref, *refs):
    means, outs = ([None] * PEERS if first else refs[:PEERS]), refs[-PEERS:]
    tokens = aligned(core(), own_ref.shape[1])
    sides = weights_of(first, own_ref)
    for part, mean_ref, out_ref in zip(SCATTER, means, outs):
        rows = rows_ref[tokens, aligned(position() ^ part, out_ref.shape[1])]
        out_ref[...] = image_term(first, *sides, rows, mean_ref)


def image_kernel(first, other_ref, rows_ref, *refs):
    *refs, weights_ref, side_ref = refs
    peers = PEERS - 1
    means, halves, outs = ([None] * peers if first else refs[:peers]), refs[-2 * peers : -peers], refs[-peers:]
    tokens = aligned(1 - core(), other_ref.shape[1])
    weights, counts, centre = weights_of(first, other_ref)
    for part, mean_ref, half_ref, out_ref in zip(SCATTER[1:], means, halves, outs):
        rows = rows_ref[tokens, aligned(position() ^ part, out_ref.shape[1])]
        out_ref[...] = half_ref[...] + image_term(first, weights, counts, centre, rows, mean_ref)
    weights_ref[...] = weights
    side_ref[...] = jnp.broadcast_to(counts, side_ref.shape)
    side_ref[:, 1:2] = centre


def own_image_kernel(first, weights_ref, side_ref, rows_ref, half_ref, *refs):
    mean_ref, out_ref = (None if first else refs[0]), refs[-1]
    tokens = aligned(1 - core(), weights_ref.shape[1])
    rows = rows_ref[tokens, aligned(position(), out_ref.shape[1])]
    sides = weights_ref[...], side_ref[:, :1], side_ref[:, 1:2]
    out_ref[...] = half_ref[...] + image_term(first, *sides, rows, mean_ref)


def assemble_kernel(*refs):
    *chunks, out_ref = refs
    width = chunks[0].shape[1]
    for part, chunk in zip(GATHER, chunks):
        out_ref[:, aligned(position() ^ part, width)] = stacked(chunk[...].astype(F32))


def last_kernel(own_ref, got_ref, lower_ref, image_ref, scores_ref, basis_ref):
    n, lower = lower_ref.shape[0], lower_ref[...]
    basis_ref[...] = product(lower, image_ref[...])
    projected = product(lower, stacked(total(own_ref, got_ref)))
    scores_ref[...] = jnp.sum(projected * projected, axis=0) / n


def normalised_total_kernel(own_ref, got_ref, lower_ref, out_ref):
    value = own_ref[...] + got_ref[...]
    out_ref[...] = product(lower_ref[...], stacked(value)).astype(out_ref.dtype)


def ordered_copy_kernel(value_ref, before_ref, out_ref):
    out_ref[...] = value_ref[...]


def ordered_add_kernel(own_ref, got_ref, before_ref, out_ref):
    out_ref[...] = total(own_ref, got_ref).astype(out_ref.dtype)


def add_kernel(*refs):
    refs[-1][...] = total(*refs[:-1]).astype(refs[-1].dtype)


def add(*terms, dtype=F32):
    return call(add_kernel, [(terms[0].shape, dtype)], "add")(*terms)[0]


def swap(value, axis, distance):
    size = lax.axis_size(axis)
    if axis == "feat" and distance > 1:
        distance += 1
    return lax.ppermute(value, axis, [(i, i ^ distance) for i in range(size)])


def distances(axis, start):
    step, size = start, lax.axis_size(axis)
    while step < size:
        yield step
        step *= 2


def share(value, axis):
    return [value] + [swap(value, axis, part) for part in GATHER[1:]]


def on_device(activations, start_basis):
    tokens, features = activations.shape
    n = start_basis.shape[0]
    width = features // PEERS
    rows_in_all = tokens * lax.axis_size("tok")
    last_feat = lax.axis_size("feat") // 2
    side = ((n, LANES), F32)
    half = ((n, tokens // 2), F32)
    whole = ((n, tokens), F32)

    fetched, sem = (activations.shape, BF16), [pltpu.SemaphoreType.DMA(())]
    rows = call(fetch_kernel, [fetched], "fetch", sem, in_specs=[HBM], mebibytes=46)(activations)[0]
    sent, rows = call(
        first_sent_kernel,
        [half, fetched],
        "sent_projection",
        sem,
        in_specs=[VMEM, HBM, VMEM],
        aliases={2: 1},
        mebibytes=46,
    )(start_basis, activations, rows)
    own = call(first_kept_kernel, [half], "kept_projection", cost=SHORT)(start_basis, rows)[0]
    for distance in distances("feat", 1):
        own = add(own, swap(sent if distance == 1 else own, "feat", distance))
    other = swap(own, "feat", 1)
    means, ranked, lower = [], [], []
    for step in range(ITERS):
        first, last = step == 0, step == ITERS - 1
        chunk = ((n + EXTRA if first else n, width), F32)
        weights = ((TERMS * n + 2 * EXTRA if first else TERMS * n, tokens // 2), BF16)
        kernel = functools.partial(half_image_kernel, first)
        kept, *halves = call(kernel, [chunk] * PEERS, "half_image", cost=SHORT)(own, rows, *ranked)
        kernel = functools.partial(image_kernel, first)
        *terms, weights, sums = call(kernel, [chunk] * (PEERS - 1) + [weights, side], "image")(
            other, rows, *ranked[1:], *halves
        )
        received = [swap(term, "tok", part) for part, term in zip(SCATTER[1:], terms)]
        kernel = functools.partial(own_image_kernel, first)
        kept = call(kernel, [chunk], "own_image", cost=SHORT)(weights, sums, rows, kept, *means[:1])
        image = add(*kept, *received)
        *steps, last_step = distances("tok", PEERS)
        for distance in steps:
            image = add(image, swap(image, "tok", distance))
        kernel = functools.partial(first_total_kernel, rows_in_all) if first else normalised_total_kernel
        image = call(kernel, [(chunk[0], BF16 if last else F32)], "total")(image, swap(image, "tok", last_step), *lower)[0]
        images = share(image, "tok")
        means = means or images
        ranked = [means[GATHER.index(part)] for part in SCATTER]
        before = []
        for part, image, mean in zip(GATHER, images, means):
            operands = [image, mean, rows, *before]
            if part != GATHER[-1]:
                kernel = functools.partial(projection_kernel, part, "all")
                before = call(kernel, [whole], "projection", cost=SHORT)(*operands)
            if part == GATHER[1]:
                ready = before if last else []
        gram = call(gram_kernel, [side], "gram")(*images, *ready)[0]
        grams = (gram, swap(gram, "feat", 1))
        if last:
            gram = add(*grams)
            kernel = functools.partial(projection_kernel, part, "all")
            own = call(kernel, [whole], "projection", cost=SHORT)(*operands)[0]
            own = call(ordered_copy_kernel, [whole], "copy")(own, gram)[0]
            for distance in distances("feat", 1):
                terms = (own, swap(own, "feat", distance))
                if distance != last_feat:
                    narrow = ((n, tokens), BF16 if distance == last_feat // 2 else F32)
                    own = call(add_kernel, [narrow], "add")(*terms)[0]
            own, other = terms
            for distance in distances("feat", 2):
                grams = (gram, swap(gram, "feat", distance))
                gram = add(*grams)
        else:
            kernel = functools.partial(projection_kernel, part, "sent")
            sent = call(kernel, [half], "sent_projection")(*operands)[0]
            kernel = functools.partial(projection_kernel, part, "kept")
            own = call(kernel, [half], "kept_projection", cost=SHORT)(*operands)[0]
            for distance in distances("feat", 1):
                got = swap(sent if distance == 1 else own, "feat", distance)
                if distance > 1:
                    gram = add(*grams)
                    grams = (gram, swap(gram, "feat", distance))
                if distance == last_feat:
                    own = call(ordered_add_kernel, [half], "add")(own, got, gram)[0]
                else:
                    own = add(own, got)
            other = swap(own, "feat", 1)
        lower = call(inverse_factor_kernel, [((n, n), F32)], "inverse_factor", cost=LONG)(*grams)
    image = call(assemble_kernel, [((6 * n, features), BF16)], "assemble")(*images)[0]
    outputs = [((tokens,), F32), ((n, features), F32)]
    return tuple(call(last_kernel, outputs, "last")(own, other, *lower, image))


def solution(mesh):
    in_specs = (P("tok", "feat"), P(None, "feat"))
    out_specs = (P("tok"), P(None, "feat"))
    return jax.shard_map(
        on_device, mesh=mesh, in_specs=in_specs, out_specs=out_specs, check_vma=False
    )
```

```python
import functools

import jax
import jax.numpy as jnp
from jax import lax
from jax.experimental import pallas as pl
from jax.experimental.pallas import tpu as pltpu
from jax.sharding import PartitionSpec as P

ITERS = 4
PEERS = 4
LANES = 128
EXTRA = 8
SCATTER = (0, 3, 1, 2)
GATHER = (0, 3, 2, 1)
TERMS = 3
LONG = pl.CostEstimate(flops=2**34, bytes_accessed=0, transcendentals=0)
SHORT = pl.CostEstimate(flops=2**29, bytes_accessed=0, transcendentals=0)
HIGHEST = lax.Precision.HIGHEST
VMEM = pl.BlockSpec(memory_space=pltpu.VMEM)
HBM = pl.BlockSpec(memory_space=pltpu.HBM)
F32 = jnp.float32
BF16 = jnp.bfloat16


def call(kernel, outputs, name, scratch=(), in_specs=None, aliases=None, mebibytes=20, cost=None):
    def run(*args):
        specs = in_specs or [VMEM] * len(args)
        return pl.pallas_call(
            kernel,
            out_shape=[jax.ShapeDtypeStruct(shape, dtype) for shape, dtype in outputs],
            in_specs=specs,
            out_specs=[VMEM] * len(outputs),
            scratch_shapes=scratch,
            compiler_params=pltpu.CompilerParams(vmem_limit_bytes=mebibytes * 2**20),
            cost_estimate=cost,
            input_output_aliases=aliases or {},
            name=name,
        )(*args)

    return run


def split(value, terms=2):
    parts = []
    for _ in range(terms):
        parts.append(value.astype(BF16))
        value = value - parts[-1].astype(F32)
    return jnp.concatenate(parts, axis=0)


def join(value, terms=2):
    height = value.shape[0] // terms
    result = value[-height:]
    for term in range(terms - 2, -1, -1):
        result = value[term * height : (term + 1) * height] + result
    return result


def total(*refs):
    terms = [ref[...].astype(F32) for ref in refs]
    while len(terms) > 1:
        terms = [sum(terms[i + 1 : i + 2], terms[i]) for i in range(0, len(terms), 2)]
    return terms[0]


def terms_of(value):
    parts = []
    for _ in range(3):
        parts.append(value.astype(BF16))
        value = value - parts[-1].astype(F32)
    return parts


def stacked(value):
    high, middle, low = terms_of(value)
    return jnp.concatenate([high, middle, low, high, middle, high], axis=0)


def product(left, right_stacked):
    high, middle, low = terms_of(left)
    left = jnp.concatenate([high, high, high, middle, middle, low], axis=1)
    return jnp.dot(left, right_stacked, preferred_element_type=F32)


def contract_last(left, right, precision=None):
    return lax.dot_general(
        left, right, (((1,), (1,)), ((), ())), preferred_element_type=F32, precision=precision
    )


def position():
    return lax.rem(lax.axis_index("tok"), PEERS)


def diagonal(n):
    return lax.broadcasted_iota(jnp.int32, (n, n), 0) == lax.broadcasted_iota(jnp.int32, (n, n), 1)


def core():
    index, parity, shift = lax.axis_index("feat"), 0, 1
    while shift < lax.axis_size("feat"):
        parity = parity + lax.rem(index // shift, 2)
        shift *= 2
    return lax.rem(parity, 2)


def aligned(index, size):
    return pl.ds(pl.multiple_of(index * size, size), size)


def fetch_kernel(rows_hbm, rows_ref, sem):
    place = aligned(1 - core(), rows_ref.shape[0] // 2)
    copy = pltpu.make_async_copy(rows_hbm.at[place, :], rows_ref.at[place, :], sem)
    copy.start()
    copy.wait()


def first_sent_kernel(basis_ref, rows_hbm, ready_ref, out_ref, rows_ref, sem):
    half = out_ref.shape[1]
    place = aligned(core(), half)
    copy = pltpu.make_async_copy(rows_hbm.at[place, :], rows_ref.at[place, :], sem)
    copy.start()
    rows = rows_ref[aligned(1 - core(), half), :]
    out_ref[...] = join(contract_last(split(basis_ref[...]), rows))
    copy.wait()


def first_kept_kernel(basis_ref, rows_ref, out_ref):
    rows = rows_ref[aligned(core(), out_ref.shape[1]), :]
    out_ref[...] = join(contract_last(split(basis_ref[...]), rows))


def projection_kernel(part, half, chunk_ref, mean_ref, rows_ref, *refs):
    out_ref = refs[-1]
    n, tokens = out_ref.shape
    place = {"all": 0, "kept": core(), "sent": 1 - core()}[half]
    place = aligned(place, tokens) if half != "all" else slice(None)
    chunk = chunk_ref[:n, :]
    shift = jnp.sum(chunk * mean_ref[n : n + 1, :], axis=1, keepdims=True)
    rows = rows_ref[place, aligned(position() ^ part, chunk.shape[1])]
    value = join(contract_last(split(chunk), rows)) - shift
    out_ref[...] = value if part == GATHER[0] else refs[0][:, place] + value


def gram_kernel(*refs):
    *refs, out_ref = refs
    n = out_ref.shape[0]
    chunks = {part: ref[:n, :] for part, ref in zip(GATHER, refs)}
    parts = [contract_last(chunks[part], chunks[part], HIGHEST) for part in range(PEERS)]
    out_ref[...] = jnp.zeros(out_ref.shape, F32)
    out_ref[:, :n] = (parts[0] + parts[1]) + (parts[2] + parts[3])


def inverse_factor_kernel(own_ref, got_ref, out_ref):
    n = own_ref.shape[0]
    gram = (own_ref[...] + got_ref[...])[:, :n]
    work = jnp.concatenate([gram, diagonal(n).astype(F32)], axis=1)
    index = lax.broadcasted_iota(jnp.int32, (n, 1), 0)
    scale = jnp.zeros((n, 1), F32)
    for k in range(n):
        pivot = work[k : k + 1, k : k + 1]
        factor = jnp.where(index > k, work[:, k : k + 1] / pivot, 0.0)
        scale = jnp.where(index == k, lax.rsqrt(pivot), scale)
        work = work - factor * work[k : k + 1, :]
    out_ref[...] = work[:, n:] * scale


def first_total_kernel(rows_in_all, own_ref, got_ref, out_ref):
    n = own_ref.shape[0] - EXTRA
    value = own_ref[...] + got_ref[...]
    mean = value[n : n + 1] / rows_in_all
    counts = jnp.where(diagonal(n), value[n + 1 : n + 2, :n], 0.0)
    counts = jnp.sum(counts, axis=1, keepdims=True)
    out_ref[:n, :] = value[:n] - counts * mean
    out_ref[n:, :] = jnp.broadcast_to(mean, (EXTRA, mean.shape[1]))


def weights_of(first, projected_ref):
    projected = projected_ref[...]
    centre = jnp.zeros((projected.shape[0], 1), F32)
    if first:
        centre = jnp.sum(projected, axis=1, keepdims=True) / projected.shape[1]
    weights = split(projected - centre if first else projected, TERMS)
    counts = join(jnp.sum(weights.astype(F32), axis=1, keepdims=True), TERMS)
    if first:
        counts = counts + centre * projected.shape[1]
        weights = jnp.concatenate([weights, jnp.ones((2 * EXTRA, projected.shape[1]), BF16)], axis=0)
    return weights, counts, centre


def image_term(first, weights, counts, centre, rows, mean_ref):
    n = counts.shape[0]
    term = jnp.dot(weights, rows, preferred_element_type=F32)
    value = join(term[: TERMS * n], TERMS)
    if not first:
        return value - counts * mean_ref[n : n + 1, :]
    sums = term[TERMS * n : TERMS * n + 1]
    counts = jnp.sum(jnp.where(diagonal(n), counts, 0.0), axis=0, keepdims=True)
    counts = jnp.concatenate([counts, jnp.zeros((1, sums.shape[1] - n), F32)], axis=1)
    below = jnp.zeros((EXTRA - 2, sums.shape[1]), F32)
    return jnp.concatenate([value + centre * sums, sums, counts, below], axis=0)


def half_image_kernel(first, own_ref, rows_ref, *refs):
    means, outs = ([None] * PEERS if first else refs[:PEERS]), refs[-PEERS:]
    tokens = aligned(core(), own_ref.shape[1])
    sides = weights_of(first, own_ref)
    for part, mean_ref, out_ref in zip(SCATTER, means, outs):
        rows = rows_ref[tokens, aligned(position() ^ part, out_ref.shape[1])]
        out_ref[...] = image_term(first, *sides, rows, mean_ref)


def image_kernel(first, other_ref, rows_ref, *refs):
    *refs, weights_ref, side_ref = refs
    peers = PEERS - 1
    means, halves, outs = ([None] * peers if first else refs[:peers]), refs[-2 * peers : -peers], refs[-peers:]
    tokens = aligned(1 - core(), other_ref.shape[1])
    weights, counts, centre = weights_of(first, other_ref)
    for part, mean_ref, half_ref, out_ref in zip(SCATTER[1:], means, halves, outs):
        rows = rows_ref[tokens, aligned(position() ^ part, out_ref.shape[1])]
        out_ref[...] = half_ref[...] + image_term(first, weights, counts, centre, rows, mean_ref)
    weights_ref[...] = weights
    side_ref[...] = jnp.broadcast_to(counts, side_ref.shape)
    side_ref[:, 1:2] = centre


def own_image_kernel(first, weights_ref, side_ref, rows_ref, half_ref, *refs):
    mean_ref, out_ref = (None if first else refs[0]), refs[-1]
    tokens = aligned(1 - core(), weights_ref.shape[1])
    rows = rows_ref[tokens, aligned(position(), out_ref.shape[1])]
    sides = weights_ref[...], side_ref[:, :1], side_ref[:, 1:2]
    out_ref[...] = half_ref[...] + image_term(first, *sides, rows, mean_ref)


def assemble_kernel(*refs):
    *chunks, out_ref = refs
    width = chunks[0].shape[1]
    for part, chunk in zip(GATHER, chunks):
        out_ref[:, aligned(position() ^ part, width)] = stacked(chunk[...])


def last_kernel(own_ref, got_ref, lower_ref, image_ref, scores_ref, basis_ref):
    n, lower = lower_ref.shape[0], lower_ref[...]
    basis_ref[...] = product(lower, image_ref[...])
    projected = product(lower, stacked(total(own_ref, got_ref)))
    scores_ref[...] = jnp.sum(projected * projected, axis=0) / n


def normalised_total_kernel(own_ref, got_ref, lower_ref, out_ref):
    value = own_ref[...] + got_ref[...]
    out_ref[...] = product(lower_ref[...], stacked(value))


def ordered_copy_kernel(value_ref, before_ref, out_ref):
    out_ref[...] = value_ref[...]


def ordered_add_kernel(own_ref, got_ref, before_ref, out_ref):
    out_ref[...] = total(own_ref, got_ref).astype(out_ref.dtype)


def add_kernel(*refs):
    refs[-1][...] = total(*refs[:-1]).astype(refs[-1].dtype)


def add(*terms, dtype=F32):
    return call(add_kernel, [(terms[0].shape, dtype)], "add")(*terms)[0]


def swap(value, axis, distance):
    size = lax.axis_size(axis)
    if axis == "feat" and distance > 1:
        distance += 1
    return lax.ppermute(value, axis, [(i, i ^ distance) for i in range(size)])


def distances(axis, start):
    step, size = start, lax.axis_size(axis)
    while step < size:
        yield step
        step *= 2


def share(value, axis):
    return [value] + [swap(value, axis, part) for part in GATHER[1:]]


def on_device(activations, start_basis):
    tokens, features = activations.shape
    n = start_basis.shape[0]
    width = features // PEERS
    rows_in_all = tokens * lax.axis_size("tok")
    last_feat = lax.axis_size("feat") // 2
    side = ((n, LANES), F32)
    half = ((n, tokens // 2), F32)
    whole = ((n, tokens), F32)

    fetched, sem = (activations.shape, BF16), [pltpu.SemaphoreType.DMA(())]
    rows = call(fetch_kernel, [fetched], "fetch", sem, in_specs=[HBM], mebibytes=46)(activations)[0]
    sent, rows = call(
        first_sent_kernel,
        [half, fetched],
        "sent_projection",
        sem,
        in_specs=[VMEM, HBM, VMEM],
        aliases={2: 1},
        mebibytes=46,
    )(start_basis, activations, rows)
    own = call(first_kept_kernel, [half], "kept_projection", cost=SHORT)(start_basis, rows)[0]
    for distance in distances("feat", 1):
        own = add(own, swap(sent if distance == 1 else own, "feat", distance))
    other = swap(own, "feat", 1)
    means, ranked, lower = [], [], []
    for step in range(ITERS):
        first, last = step == 0, step == ITERS - 1
        chunk = ((n + EXTRA if first else n, width), F32)
        weights = ((TERMS * n + 2 * EXTRA if first else TERMS * n, tokens // 2), BF16)
        kernel = functools.partial(half_image_kernel, first)
        kept, *halves = call(kernel, [chunk] * PEERS, "half_image", cost=SHORT)(own, rows, *ranked)
        kernel = functools.partial(image_kernel, first)
        *terms, weights, sums = call(kernel, [chunk] * (PEERS - 1) + [weights, side], "image")(
            other, rows, *ranked[1:], *halves
        )
        received = [swap(term, "tok", part) for part, term in zip(SCATTER[1:], terms)]
        kernel = functools.partial(own_image_kernel, first)
        kept = call(kernel, [chunk], "own_image", cost=SHORT)(weights, sums, rows, kept, *means[:1])
        image = add(*kept, *received)
        *steps, last_step = distances("tok", PEERS)
        for distance in steps:
            image = add(image, swap(image, "tok", distance))
        kernel = functools.partial(first_total_kernel, rows_in_all) if first else normalised_total_kernel
        image = call(kernel, [chunk], "total")(image, swap(image, "tok", last_step), *lower)[0]
        images = share(image, "tok")
        means = means or images
        ranked = [means[GATHER.index(part)] for part in SCATTER]
        before = []
        for part, image, mean in zip(GATHER, images, means):
            operands = [image, mean, rows, *before]
            if part != GATHER[-1]:
                kernel = functools.partial(projection_kernel, part, "all")
                before = call(kernel, [whole], "projection", cost=SHORT)(*operands)
            if part == GATHER[1]:
                ready = before if last else []
        gram = call(gram_kernel, [side], "gram")(*images, *ready)[0]
        grams = (gram, swap(gram, "feat", 1))
        if last:
            gram = add(*grams)
            kernel = functools.partial(projection_kernel, part, "all")
            own = call(kernel, [whole], "projection", cost=SHORT)(*operands)[0]
            own = call(ordered_copy_kernel, [whole], "copy")(own, gram)[0]
            for distance in distances("feat", 1):
                terms = (own, swap(own, "feat", distance))
                if distance != last_feat:
                    narrow = ((n, tokens), BF16 if distance == last_feat // 2 else F32)
                    own = call(add_kernel, [narrow], "add")(*terms)[0]
            own, other = terms
            for distance in distances("feat", 2):
                grams = (gram, swap(gram, "feat", distance))
                gram = add(*grams)
        else:
            kernel = functools.partial(projection_kernel, part, "sent")
            sent = call(kernel, [half], "sent_projection")(*operands)[0]
            kernel = functools.partial(projection_kernel, part, "kept")
            own = call(kernel, [half], "kept_projection", cost=SHORT)(*operands)[0]
            for distance in distances("feat", 1):
                got = swap(sent if distance == 1 else own, "feat", distance)
                if distance > 1:
                    gram = add(*grams)
                    grams = (gram, swap(gram, "feat", distance))
                if distance == last_feat:
                    own = call(ordered_add_kernel, [half], "add")(own, got, gram)[0]
                else:
                    own = add(own, got)
            other = swap(own, "feat", 1)
        lower = call(inverse_factor_kernel, [((n, n), F32)], "inverse_factor", cost=LONG)(*grams)
    image = call(assemble_kernel, [((6 * n, features), BF16)], "assemble")(*images)[0]
    outputs = [((tokens,), F32), ((n, features), F32)]
    return tuple(call(last_kernel, outputs, "last")(own, other, *lower, image))


def solution(mesh):
    in_specs = (P("tok", "feat"), P(None, "feat"))
    out_specs = (P("tok"), P(None, "feat"))
    return jax.shard_map(
        on_device, mesh=mesh, in_specs=in_specs, out_specs=out_specs, check_vma=False
    )
```

```python
import functools

import jax
import jax.numpy as jnp
from jax import lax
from jax.experimental import pallas as pl
from jax.experimental.pallas import tpu as pltpu
from jax.sharding import PartitionSpec as P

ITERS = 4
PEERS = 4
LANES = 128
EXTRA = 8
SCATTER = (0, 3, 1, 2)
GATHER = (0, 3, 2, 1)
TERMS = 3
LONG = pl.CostEstimate(flops=2**34, bytes_accessed=0, transcendentals=0)
SHORT = pl.CostEstimate(flops=2**29, bytes_accessed=0, transcendentals=0)
HIGHEST = lax.Precision.HIGHEST
VMEM = pl.BlockSpec(memory_space=pltpu.VMEM)
HBM = pl.BlockSpec(memory_space=pltpu.HBM)
F32 = jnp.float32
BF16 = jnp.bfloat16


def call(kernel, outputs, name, scratch=(), in_specs=None, aliases=None, mebibytes=20, cost=None):
    def run(*args):
        specs = in_specs or [VMEM] * len(args)
        return pl.pallas_call(
            kernel,
            out_shape=[jax.ShapeDtypeStruct(shape, dtype) for shape, dtype in outputs],
            in_specs=specs,
            out_specs=[VMEM] * len(outputs),
            scratch_shapes=scratch,
            compiler_params=pltpu.CompilerParams(vmem_limit_bytes=mebibytes * 2**20),
            cost_estimate=cost,
            input_output_aliases=aliases or {},
            name=name,
        )(*args)

    return run


def split(value, terms=2):
    parts = []
    for _ in range(terms):
        parts.append(value.astype(BF16))
        value = value - parts[-1].astype(F32)
    return jnp.concatenate(parts, axis=0)


def join(value, terms=2):
    height = value.shape[0] // terms
    result = value[-height:]
    for term in range(terms - 2, -1, -1):
        result = value[term * height : (term + 1) * height] + result
    return result


def total(*refs):
    terms = [ref[...].astype(F32) for ref in refs]
    while len(terms) > 1:
        terms = [sum(terms[i + 1 : i + 2], terms[i]) for i in range(0, len(terms), 2)]
    return terms[0]


def terms_of(value):
    parts = []
    for _ in range(3):
        parts.append(value.astype(BF16))
        value = value - parts[-1].astype(F32)
    return parts


def stacked(value):
    high, middle, low = terms_of(value)
    return jnp.concatenate([high, middle, low, high, middle, high], axis=0)


def product(left, right_stacked):
    high, middle, low = terms_of(left)
    left = jnp.concatenate([high, high, high, middle, middle, low], axis=1)
    return jnp.dot(left, right_stacked, preferred_element_type=F32)


def contract_last(left, right, precision=None):
    return lax.dot_general(
        left, right, (((1,), (1,)), ((), ())), preferred_element_type=F32, precision=precision
    )


def position():
    return lax.rem(lax.axis_index("tok"), PEERS)


def diagonal(n):
    return lax.broadcasted_iota(jnp.int32, (n, n), 0) == lax.broadcasted_iota(jnp.int32, (n, n), 1)


def core():
    index, parity, shift = lax.axis_index("feat"), 0, 1
    while shift < lax.axis_size("feat"):
        parity = parity + lax.rem(index // shift, 2)
        shift *= 2
    return lax.rem(parity, 2)


def aligned(index, size):
    return pl.ds(pl.multiple_of(index * size, size), size)


def fetch_kernel(rows_hbm, rows_ref, sem):
    place = aligned(1 - core(), rows_ref.shape[0] // 2)
    copy = pltpu.make_async_copy(rows_hbm.at[place, :], rows_ref.at[place, :], sem)
    copy.start()
    copy.wait()


def first_sent_kernel(basis_ref, rows_hbm, ready_ref, out_ref, rows_ref, sem):
    half = out_ref.shape[1]
    place = aligned(core(), half)
    copy = pltpu.make_async_copy(rows_hbm.at[place, :], rows_ref.at[place, :], sem)
    copy.start()
    rows = rows_ref[aligned(1 - core(), half), :]
    out_ref[...] = join(contract_last(split(basis_ref[...]), rows))
    copy.wait()


def first_kept_kernel(basis_ref, rows_ref, out_ref):
    rows = rows_ref[aligned(core(), out_ref.shape[1]), :]
    out_ref[...] = join(contract_last(split(basis_ref[...]), rows))


def projection_kernel(part, half, chunk_ref, mean_ref, rows_ref, *refs):
    out_ref = refs[-1]
    n, tokens = out_ref.shape
    place = {"all": 0, "kept": core(), "sent": 1 - core()}[half]
    place = aligned(place, tokens) if half != "all" else slice(None)
    chunk = chunk_ref[:n, :]
    shift = jnp.sum(chunk * mean_ref[n : n + 1, :], axis=1, keepdims=True)
    rows = rows_ref[place, aligned(position() ^ part, chunk.shape[1])]
    value = join(contract_last(split(chunk), rows)) - shift
    out_ref[...] = value if part == GATHER[0] else refs[0][:, place] + value


def gram_kernel(*refs):
    *refs, out_ref = refs
    n = out_ref.shape[0]
    chunks = {part: ref[:n, :] for part, ref in zip(GATHER, refs)}
    parts = [contract_last(chunks[part], chunks[part], HIGHEST) for part in range(PEERS)]
    out_ref[...] = jnp.zeros(out_ref.shape, F32)
    out_ref[:, :n] = (parts[0] + parts[1]) + (parts[2] + parts[3])


def inverse_factor_kernel(own_ref, got_ref, out_ref):
    n = own_ref.shape[0]
    gram = (own_ref[...] + got_ref[...])[:, :n]
    work = jnp.concatenate([gram, diagonal(n).astype(F32)], axis=1)
    index = lax.broadcasted_iota(jnp.int32, (n, 1), 0)
    scale = jnp.zeros((n, 1), F32)
    for k in range(n):
        pivot = work[k : k + 1, k : k + 1]
        factor = jnp.where(index > k, work[:, k : k + 1] / pivot, 0.0)
        scale = jnp.where(index == k, lax.rsqrt(pivot), scale)
        work = work - factor * work[k : k + 1, :]
    out_ref[...] = work[:, n:] * scale


def first_total_kernel(rows_in_all, own_ref, got_ref, out_ref):
    n = own_ref.shape[0] - EXTRA
    value = own_ref[...] + got_ref[...]
    mean = value[n : n + 1] / rows_in_all
    counts = jnp.where(diagonal(n), value[n + 1 : n + 2, :n], 0.0)
    counts = jnp.sum(counts, axis=1, keepdims=True)
    out_ref[:n, :] = value[:n] - counts * mean
    out_ref[n:, :] = jnp.broadcast_to(mean, (EXTRA, mean.shape[1]))


def weights_of(first, projected_ref):
    projected = projected_ref[...]
    centre = jnp.zeros((projected.shape[0], 1), F32)
    if first:
        centre = jnp.sum(projected, axis=1, keepdims=True) / projected.shape[1]
    weights = split(projected - centre if first else projected, TERMS)
    counts = join(jnp.sum(weights.astype(F32), axis=1, keepdims=True), TERMS)
    if first:
        counts = counts + centre * projected.shape[1]
        weights = jnp.concatenate([weights, jnp.ones((2 * EXTRA, projected.shape[1]), BF16)], axis=0)
    return weights, counts, centre


def image_term(first, weights, counts, centre, rows, mean_ref):
    n = counts.shape[0]
    term = jnp.dot(weights, rows, preferred_element_type=F32)
    value = join(term[: TERMS * n], TERMS)
    if not first:
        return value - counts * mean_ref[n : n + 1, :]
    sums = term[TERMS * n : TERMS * n + 1]
    counts = jnp.sum(jnp.where(diagonal(n), counts, 0.0), axis=0, keepdims=True)
    counts = jnp.concatenate([counts, jnp.zeros((1, sums.shape[1] - n), F32)], axis=1)
    below = jnp.zeros((EXTRA - 2, sums.shape[1]), F32)
    return jnp.concatenate([value + centre * sums, sums, counts, below], axis=0)


def half_image_kernel(first, own_ref, rows_ref, *refs):
    means, outs = ([None] * PEERS if first else refs[:PEERS]), refs[-PEERS:]
    tokens = aligned(core(), own_ref.shape[1])
    sides = weights_of(first, own_ref)
    for part, mean_ref, out_ref in zip(SCATTER, means, outs):
        rows = rows_ref[tokens, aligned(position() ^ part, out_ref.shape[1])]
        out_ref[...] = image_term(first, *sides, rows, mean_ref)


def image_kernel(first, other_ref, rows_ref, *refs):
    *refs, weights_ref, side_ref = refs
    peers = PEERS - 1
    means, halves, outs = ([None] * peers if first else refs[:peers]), refs[-2 * peers : -peers], refs[-peers:]
    tokens = aligned(1 - core(), other_ref.shape[1])
    weights, counts, centre = weights_of(first, other_ref)
    for part, mean_ref, half_ref, out_ref in zip(SCATTER[1:], means, halves, outs):
        rows = rows_ref[tokens, aligned(position() ^ part, out_ref.shape[1])]
        out_ref[...] = half_ref[...] + image_term(first, weights, counts, centre, rows, mean_ref)
    weights_ref[...] = weights
    side_ref[...] = jnp.broadcast_to(counts, side_ref.shape)
    side_ref[:, 1:2] = centre


def own_image_kernel(first, weights_ref, side_ref, rows_ref, half_ref, *refs):
    mean_ref, out_ref = (None if first else refs[0]), refs[-1]
    tokens = aligned(1 - core(), weights_ref.shape[1])
    rows = rows_ref[tokens, aligned(position(), out_ref.shape[1])]
    sides = weights_ref[...], side_ref[:, :1], side_ref[:, 1:2]
    out_ref[...] = half_ref[...] + image_term(first, *sides, rows, mean_ref)


def assemble_kernel(*refs):
    *chunks, out_ref = refs
    width = chunks[0].shape[1]
    for part, chunk in zip(GATHER, chunks):
        out_ref[:, aligned(position() ^ part, width)] = stacked(chunk[...])


def last_kernel(own_ref, got_ref, lower_ref, image_ref, scores_ref, basis_ref):
    n, lower = lower_ref.shape[0], lower_ref[...]
    basis_ref[...] = product(lower, image_ref[...])
    projected = product(lower, stacked(total(own_ref, got_ref)))
    scores_ref[...] = jnp.sum(projected * projected, axis=0) / n


def normalised_total_kernel(own_ref, got_ref, lower_ref, out_ref):
    value = own_ref[...] + got_ref[...]
    out_ref[...] = product(lower_ref[...], stacked(value))


def ordered_copy_kernel(value_ref, before_ref, out_ref):
    out_ref[...] = value_ref[...]


def ordered_add_kernel(own_ref, got_ref, before_ref, out_ref):
    out_ref[...] = total(own_ref, got_ref).astype(out_ref.dtype)


def add_kernel(*refs):
    refs[-1][...] = total(*refs[:-1]).astype(refs[-1].dtype)


def add(*terms, dtype=F32):
    return call(add_kernel, [(terms[0].shape, dtype)], "add")(*terms)[0]


def swap(value, axis, distance):
    size = lax.axis_size(axis)
    if axis == "feat" and distance > 1:
        distance += 1
    return lax.ppermute(value, axis, [(i, i ^ distance) for i in range(size)])


def distances(axis, start):
    step, size = start, lax.axis_size(axis)
    while step < size:
        yield step
        step *= 2


def share(value, axis):
    return [value] + [swap(value, axis, part) for part in GATHER[1:]]


def on_device(activations, start_basis):
    tokens, features = activations.shape
    n = start_basis.shape[0]
    width = features // PEERS
    rows_in_all = tokens * lax.axis_size("tok")
    last_feat = lax.axis_size("feat") // 2
    side = ((n, LANES), F32)
    half = ((n, tokens // 2), F32)
    whole = ((n, tokens), F32)

    fetched, sem = (activations.shape, BF16), [pltpu.SemaphoreType.DMA(())]
    rows = call(fetch_kernel, [fetched], "fetch", sem, in_specs=[HBM], mebibytes=46)(activations)[0]
    sent, rows = call(
        first_sent_kernel,
        [half, fetched],
        "sent_projection",
        sem,
        in_specs=[VMEM, HBM, VMEM],
        aliases={2: 1},
        mebibytes=46,
    )(start_basis, activations, rows)
    own = call(first_kept_kernel, [half], "kept_projection", cost=SHORT)(start_basis, rows)[0]
    for distance in distances("feat", 1):
        own = add(own, swap(sent if distance == 1 else own, "feat", distance))
    other = swap(own, "feat", 1)
    means, ranked, lower = [], [], []
    for step in range(ITERS):
        first, last = step == 0, step == ITERS - 1
        chunk = ((n + EXTRA if first else n, width), F32)
        weights = ((TERMS * n + 2 * EXTRA if first else TERMS * n, tokens // 2), BF16)
        kernel = functools.partial(half_image_kernel, first)
        kept, *halves = call(kernel, [chunk] * PEERS, "half_image", cost=LONG)(own, rows, *ranked)
        kernel = functools.partial(image_kernel, first)
        *terms, weights, sums = call(kernel, [chunk] * (PEERS - 1) + [weights, side], "image")(
            other, rows, *ranked[1:], *halves
        )
        received = [swap(term, "tok", part) for part, term in zip(SCATTER[1:], terms)]
        kernel = functools.partial(own_image_kernel, first)
        kept = call(kernel, [chunk], "own_image", cost=SHORT)(weights, sums, rows, kept, *means[:1])
        image = add(*kept, *received)
        *steps, last_step = distances("tok", PEERS)
        for distance in steps:
            image = add(image, swap(image, "tok", distance))
        kernel = functools.partial(first_total_kernel, rows_in_all) if first else normalised_total_kernel
        image = call(kernel, [chunk], "total")(image, swap(image, "tok", last_step), *lower)[0]
        images = share(image, "tok")
        means = means or images
        ranked = [means[GATHER.index(part)] for part in SCATTER]
        before = []
        for part, image, mean in zip(GATHER, images, means):
            operands = [image, mean, rows, *before]
            if part != GATHER[-1]:
                kernel = functools.partial(projection_kernel, part, "all")
                before = call(kernel, [whole], "projection", cost=SHORT)(*operands)
            if part == GATHER[1]:
                ready = before if last else []
        gram = call(gram_kernel, [side], "gram")(*images, *ready)[0]
        grams = (gram, swap(gram, "feat", 1))
        if last:
            gram = add(*grams)
            kernel = functools.partial(projection_kernel, part, "all")
            own = call(kernel, [whole], "projection", cost=SHORT)(*operands)[0]
            own = call(ordered_copy_kernel, [whole], "copy")(own, gram)[0]
            for distance in distances("feat", 1):
                terms = (own, swap(own, "feat", distance))
                if distance != last_feat:
                    narrow = ((n, tokens), BF16 if distance == last_feat // 2 else F32)
                    own = call(add_kernel, [narrow], "add")(*terms)[0]
            own, other = terms
            for distance in distances("feat", 2):
                grams = (gram, swap(gram, "feat", distance))
                gram = add(*grams)
        else:
            kernel = functools.partial(projection_kernel, part, "sent")
            sent = call(kernel, [half], "sent_projection")(*operands)[0]
            kernel = functools.partial(projection_kernel, part, "kept")
            own = call(kernel, [half], "kept_projection", cost=SHORT)(*operands)[0]
            for distance in distances("feat", 1):
                got = swap(sent if distance == 1 else own, "feat", distance)
                if distance > 1:
                    gram = add(*grams)
                    grams = (gram, swap(gram, "feat", distance))
                if distance == last_feat:
                    own = call(ordered_add_kernel, [half], "add")(own, got, gram)[0]
                else:
                    own = add(own, got)
            other = swap(own, "feat", 1)
        lower = call(inverse_factor_kernel, [((n, n), F32)], "inverse_factor", cost=LONG)(*grams)
    image = call(assemble_kernel, [((6 * n, features), BF16)], "assemble")(*images)[0]
    outputs = [((tokens,), F32), ((n, features), F32)]
    return tuple(call(last_kernel, outputs, "last")(own, other, *lower, image))


def solution(mesh):
    in_specs = (P("tok", "feat"), P(None, "feat"))
    out_specs = (P("tok"), P(None, "feat"))
    return jax.shard_map(
        on_device, mesh=mesh, in_specs=in_specs, out_specs=out_specs, check_vma=False
    )
```
